32 devices in a mesh: groups: 2 (over x), nodes: 16 (over z, y, core).
Axes of the slice: x: 2, y: 2, z: 4, core: 2. Of those that a mesh axis runs over, the one named last changes fastest.
Arguments:
- node_feats: bfloat16 [8192, 256], P(('groups', 'nodes')), parts along dimension 0, may hold values from -6 to 6
- norm_gain: float32 [256], replicated, may hold values from 0.1 to 1.9
- w_query: bfloat16 [256, 256], replicated, may hold values from -0.375 to 0.375
- w_key: bfloat16 [256, 256], replicated, may hold values from -0.375 to 0.375
- w_value: bfloat16 [256, 256], replicated, may hold values from -0.375 to 0.375
- w_out: bfloat16 [256, 256], replicated, may hold values from -0.375 to 0.375
- cotangent: bfloat16 [8192, 256], P(('groups', 'nodes')), parts along dimension 0, may hold values from -6 to 6
- edge_dst: int32 [1536, 128], P(('groups', 'nodes')), parts along dimension 0, may hold values from 0 to 255
- edge_src: int32 [1536, 128], P(('groups', 'nodes')), parts along dimension 0, may hold values from 0 to 319, as said below
- edge_mask: int32 [1536, 128], P(('groups', 'nodes')), parts along dimension 0, may hold values from 0 to 1, as said below
- send_rows: int32 [32, 16, 4], P(('groups', 'nodes')), parts along dimension 0, may hold values from 0 to 255
Outputs:
- output: bfloat16 [8192, 256], P(('groups', 'nodes')), parts along dimension 0
- grad_feats: float32 [8192, 256], P(('groups', 'nodes')), parts along dimension 0
- grad_gain: float32 [512], P('groups'), parts along dimension 0
- grad_query: float32 [512, 256], P('groups'), parts along dimension 0
- grad_key: float32 [512, 256], P('groups'), parts along dimension 0
- grad_value: float32 [512, 256], P('groups'), parts along dimension 0
- grad_out: float32 [512, 256], P('groups'), parts along dimension 0
The draws below stay inside these ranges and needn't reach their ends.
There are 2 independent parts, one for each index of `groups`. The reference program is written for one: setup_inputs(seed, part) draws one part's arguments, and reference() takes and returns one part's arrays. A program takes and returns all parts, laid end to end along the dimension named above; an argument that names none is the same for every part. Nothing has to cross between parts.
Inputs may be any that keep to these rules, and one draw needn't show every extreme that they name: `edge_src`: an index below 256 is a row of the same partition; 256 + s * 4 + c is slot c of the rows that partition s sends to this one. `edge_mask`: within each partition the edges fill its 48 blocks from the front; on at least one partition every slot holds an edge. `send_rows`: entry [s, p, c] is the row of partition s that it sends to partition p in slot c.
All inputs are finite; a program needn't handle non-finite values.
Results may differ from the reference program's by a relative error of at most 0.012.
Values may be sent and summed in bfloat16 or wider, within the bound.
No kernel may reach another device: no remote copies, remote signals or barrier semaphores. Data moves between devices by JAX's collectives and lax.ppermute only.
A program may use at most 64 MiB of HBM per device.

```python
import math
import jax
import jax.numpy as jnp
from jax import lax

D = 256
HEADS = 8
NODE_DEV = 256
CAP = 4
EB = 48
NODES = 4096
N_NODES = 16


def edge_draw(key):
    load_key, target_key, source_key, remote_key, kind_key, busy_key = jax.random.split(key, 6)
    slot_total = EB * 128
    load_level = jax.random.randint(load_key, (N_NODES,), 2, 17)
    counts = slot_total * load_level * load_level // 256
    busiest = jax.random.randint(busy_key, (), 0, N_NODES)
    counts = jnp.where(jnp.arange(N_NODES) == busiest, slot_total, counts)
    position = jnp.arange(slot_total)[None, :]
    validity = (position < counts[:, None]).astype(jnp.int32).reshape(N_NODES * EB, 128)
    edge_shape = (N_NODES * EB, 128)
    targets = jax.random.randint(target_key, edge_shape, 0, NODE_DEV)
    nearby = jax.random.randint(source_key, edge_shape, 0, NODE_DEV)
    remote = jax.random.randint(remote_key, edge_shape, NODE_DEV, NODE_DEV + N_NODES * CAP)
    edge_kind = jax.random.randint(kind_key, edge_shape, 0, 2)
    sources = jnp.where(edge_kind == 0, nearby, remote)
    return (targets.astype(jnp.int32), sources.astype(jnp.int32), validity)


def draw_edge_dst(key, part):
    return edge_draw(key)[0]


def draw_edge_src(key, part):
    return edge_draw(key)[1]


def draw_edge_mask(key, part):
    return edge_draw(key)[2]


def with_ends(entries, own_key, low, largest):
    extent = entries.shape
    spot = [jax.random.randint(jax.random.fold_in(own_key, axis), (), 0, extent[axis]) for axis in range(len(extent))]
    entries = entries.at[tuple(spot)].set(low)
    longest = extent.index(max(extent))
    spot[longest] = (spot[longest] + 1) % extent[longest]
    return entries.at[tuple(spot)].set(largest)


def level_of(stream_key, extent, cuts, smallest, largest):
    def one(dim, shards_of):
        heights = jax.random.uniform(jax.random.fold_in(jax.random.fold_in(stream_key, 6), dim), (shards_of,), jnp.float32, smallest / len(cuts), largest / len(cuts))
        return jnp.repeat(jnp.exp(heights), extent[dim] // shards_of).reshape((-1,) + (1,) * (len(extent) - dim - 1))

    level = one(*cuts[0])
    for cut in cuts[1:]:
        level = level * one(*cut)
    return level


def normal_values(key, extent, deviation, most, pieces=(), kind=jnp.bfloat16):
    loudness = level_of(key, extent, pieces, -0.22, 0.18) if pieces else 1.0
    entries = jax.random.normal(key, extent, jnp.float32) * deviation * loudness
    return jnp.minimum(jnp.maximum(entries, -most), most).astype(kind)


def setup_inputs(seed: int = 0, part: int = 0) -> dict:
    key_list = jax.random.split(jax.random.key(seed), 12)
    part_keys = jax.random.split(jax.random.fold_in(key_list[11], part), 12)
    node_feats = normal_values(part_keys[0], (NODES, D), 1.0, 6.0, ((0, 16),))
    norm_gain = jnp.clip(1.0 + 0.18 * jax.random.normal(key_list[1], (D,), jnp.float32), 0.1, 1.9)
    w_query = normal_values(key_list[2], (D, D), D ** -0.5, 0.375)
    w_key = normal_values(key_list[3], (D, D), D ** -0.5, 0.375)
    w_value = normal_values(key_list[4], (D, D), D ** -0.5, 0.375)
    w_out = normal_values(key_list[5], (D, D), D ** -0.5, 0.375)
    cotangent = normal_values(part_keys[6], (NODES, D), 1.0, 6.0, ((0, 16),))
    edge_dst = draw_edge_dst(jax.random.fold_in(jax.random.fold_in(key_list[11], part), 71), part)
    edge_src = draw_edge_src(jax.random.fold_in(jax.random.fold_in(key_list[11], part), 71), part)
    edge_mask = draw_edge_mask(jax.random.fold_in(jax.random.fold_in(key_list[11], part), 71), part)
    send_rows = with_ends(jax.random.randint(part_keys[10], (N_NODES, N_NODES, CAP), 0, NODE_DEV), jax.random.fold_in(part_keys[10], 1), 0, NODE_DEV - 1).astype(jnp.int32)
    return dict(node_feats=node_feats, norm_gain=norm_gain, w_query=w_query, w_key=w_key, w_value=w_value, w_out=w_out, cotangent=cotangent, edge_dst=edge_dst, edge_src=edge_src, edge_mask=edge_mask, send_rows=send_rows)


def layer_norm(feats, norm_gain):
    average = lax.optimization_barrier(jnp.mean(feats, axis=1, keepdims=True))
    centered = feats - average
    variance = lax.optimization_barrier(jnp.mean(centered * centered, axis=1, keepdims=True))
    return centered * lax.rsqrt(variance + 1e-05) * norm_gain

def block_terms(query_rows, pair_rows, validity, head_count):
    features = query_rows.shape[1]
    head_size = features // head_count
    key_rows = pair_rows[:, :features]
    value_rows = pair_rows[:, features:]
    logits = lax.optimization_barrier(jnp.sum((query_rows * key_rows).reshape(-1, head_count, head_size), axis=2)) / math.sqrt(head_size)
    weight = jnp.exp(5.0 * jnp.tanh(logits / 5.0)) * validity[:, None]
    numerator = (weight[:, :, None] * value_rows.reshape(-1, head_count, head_size)).reshape(-1, features)
    return (numerator, weight)

def reference(node_feats, norm_gain, w_query, w_key, w_value, w_out, cotangent, edge_dst, edge_src, edge_mask, send_rows):
    head_size = D // HEADS
    highest = lax.Precision.HIGHEST
    feats32 = node_feats.astype(jnp.float32)
    normed = layer_norm(feats32, norm_gain).astype(jnp.bfloat16)
    queries = jnp.dot(normed, w_query, preferred_element_type=jnp.float32).astype(jnp.bfloat16)
    keys = jnp.dot(normed, w_key, preferred_element_type=jnp.float32).astype(jnp.bfloat16)
    values = jnp.dot(normed, w_value, preferred_element_type=jnp.float32).astype(jnp.bfloat16)
    query32 = queries.astype(jnp.float32)
    pair32 = jnp.concatenate([keys, values], axis=1).astype(jnp.float32)
    unit_mask = jnp.ones((NODES,), jnp.float32)
    num_self, den_self = block_terms(query32, pair32, unit_mask, HEADS)
    target_parts = edge_dst.reshape(N_NODES, EB * 128).astype(jnp.int32)
    source_parts = edge_src.reshape(N_NODES, EB * 128).astype(jnp.int32)
    valid_parts = edge_mask.reshape(N_NODES, EB * 128).astype(jnp.float32)
    part_ids = jnp.arange(N_NODES, dtype=jnp.int32)

    def global_index(partition, targets, sources):
        base_row = partition * NODE_DEV
        offset = jnp.maximum(sources - NODE_DEV, 0)
        sender = offset // CAP
        slot_index = offset % CAP
        far_row = sender * NODE_DEV + send_rows[sender, partition, slot_index]
        near_row = base_row + sources
        return ((base_row + targets).astype(jnp.int32), jnp.where(sources < NODE_DEV, near_row, far_row).astype(jnp.int32))

    def forward_part(running, item):
        numerator, denominator = running
        partition, targets, sources, validity = item
        gtarget, gsource = global_index(partition, targets, sources)
        num_part, den_part = block_terms(query32[gtarget], pair32[gsource], validity, HEADS)
        return ((numerator.at[gtarget].add(num_part), denominator.at[gtarget].add(den_part)), None)
    (numerator, denominator), _ = lax.scan(forward_part, (num_self, den_self), (part_ids, target_parts, source_parts, valid_parts))
    den_wide = jnp.repeat(denominator, head_size, axis=1)
    attended32 = numerator / den_wide
    attended = attended32.astype(jnp.bfloat16)
    output = (feats32 + jnp.dot(attended, w_out, preferred_element_type=jnp.float32)).astype(jnp.bfloat16)
    grad_out = jnp.dot(attended.T, cotangent, preferred_element_type=jnp.float32)
    d_attended = jnp.dot(cotangent, w_out.T, preferred_element_type=jnp.float32).astype(jnp.bfloat16).astype(jnp.float32)
    d_num = d_attended / den_wide
    d_den = -lax.optimization_barrier(jnp.sum((d_attended * attended32).reshape(NODES, HEADS, head_size), axis=2)) / denominator

    def self_terms(query_rows, pair_rows):
        return block_terms(query_rows, pair_rows, unit_mask, HEADS)
    _, pullback = jax.vjp(self_terms, query32, pair32)
    dq_self, dpair_self = pullback((d_num, d_den))

    def backward_part(running, item):
        dq_acc, dpair_acc = running
        partition, targets, sources, validity = item
        gtarget, gsource = global_index(partition, targets, sources)

        def edge_terms(query_rows, pair_rows):
            return block_terms(query_rows, pair_rows, validity, HEADS)
        _, pull_edges = jax.vjp(edge_terms, query32[gtarget], pair32[gsource])
        dq_rows, dpair_rows = pull_edges((d_num[gtarget], d_den[gtarget]))
        return ((dq_acc.at[gtarget].add(dq_rows), dpair_acc.at[gsource].add(dpair_rows)), None)
    (dq_acc, dpair_acc), _ = lax.scan(backward_part, (dq_self, dpair_self), (part_ids, target_parts, source_parts, valid_parts))
    dq_low = dq_acc.astype(jnp.bfloat16)
    normed32 = normed.astype(jnp.float32)
    w_pair32 = jnp.concatenate([w_key, w_value], axis=1).astype(jnp.float32)
    grad_query = jnp.dot(normed.T, dq_low, preferred_element_type=jnp.float32)
    grad_pair = jnp.dot(normed32.T, dpair_acc, precision=highest)
    grad_key = grad_pair[:, :D]
    grad_value = grad_pair[:, D:]
    d_normed = jnp.dot(dq_low, w_query.T, preferred_element_type=jnp.float32)
    d_normed = d_normed + jnp.dot(dpair_acc, w_pair32.T, precision=highest)
    _, pull_norm = jax.vjp(layer_norm, feats32, norm_gain)
    dx_norm, grad_gain = pull_norm(d_normed)
    grad_feats = cotangent.astype(jnp.float32) + dx_norm
    return (output, grad_feats, grad_gain, grad_query, grad_key, grad_value, grad_out)
```

```python
import functools
import math

import jax
import jax.numpy as jnp
from jax import lax
from jax.experimental import pallas as pl
from jax.experimental.pallas import tpu as pltpu
from jax.sharding import PartitionSpec as P

HEADS = 8
EPS = 1e-05
F32 = jnp.float32
BF16 = jnp.bfloat16
VMEM = pl.BlockSpec(memory_space=pltpu.VMEM)
SMEM = pl.BlockSpec(memory_space=pltpu.SMEM)
LIMIT = 40 * 1024 * 1024


def up(n, m):
    return -(-n // m) * m


def dot(a, b):
    return jnp.dot(a, b, preferred_element_type=F32)


def dot_t(a, b):
    return lax.dot_general(a, b, (((1,), (1,)), ((), ())), preferred_element_type=F32)


def standardize(x):
    centered = x - jnp.mean(x, axis=1, keepdims=True)
    rstd = lax.rsqrt(jnp.mean(centered * centered, axis=1, keepdims=True) + EPS)
    return centered * rstd, rstd


def pick_kernel(send_ref, feats_ref, out_ref, wide, picked):
    peers, slots = send_ref.shape
    wide[...] = feats_ref[...].astype(F32)

    def one_peer(peer, carry):
        for slot in range(slots):
            picked[pl.ds(peer * slots + slot, 1), :] = wide[pl.ds(send_ref[peer, slot], 1), :]
        return carry

    lax.fori_loop(0, peers, one_peer, 0)
    out_ref[...] = picked[...].astype(BF16)


def local_kernel(
    x_ref, gain_ref, wq_ref, wk_ref, wv_ref, wo_ref, cot_ref, dst_ref, src_ref, mask_ref,
    q_ref, k_ref, v_ref, qt_ref, normt_ref, datt_ref, count_ref,
):
    rows = x_ref.shape[0]
    width = count_ref.shape[1]
    xhat, _ = standardize(x_ref[...].astype(F32))
    normed = (xhat * gain_ref[...]).astype(BF16)
    q = dot(normed, wq_ref[...]).astype(BF16)
    q_ref[...] = q
    qt_ref[...] = q.T
    normt_ref[...] = normed.T
    k_ref[...] = dot(normed, wk_ref[...]).astype(BF16)
    v_ref[...] = dot(normed, wv_ref[...]).astype(BF16)
    datt_ref[...] = dot_t(cot_ref[...], wo_ref[...]).astype(BF16)
    row_id = lax.broadcasted_iota(jnp.int32, (rows, width), 0)
    col_id = lax.broadcasted_iota(jnp.int32, (rows, width), 1)
    count_ref[...] = (row_id == col_id).astype(F32)
    group = 8
    edge = 128
    dst_id = lax.broadcasted_iota(jnp.int32, (rows, edge), 0)
    src_id = lax.broadcasted_iota(jnp.int32, (width, edge), 0)

    def step(i, carry):
        base = pl.multiple_of(i * group, group)
        dst = dst_ref[pl.ds(base, group), :]
        src = jnp.where(mask_ref[pl.ds(base, group), :] > 0, src_ref[pl.ds(base, group), :], -1)
        hot_dst = jnp.concatenate(
            [(dst_id == dst[j : j + 1]).astype(F32).astype(BF16) for j in range(group)], axis=1
        )
        hot_src = jnp.concatenate(
            [(src_id == src[j : j + 1]).astype(F32).astype(BF16) for j in range(group)], axis=1
        )
        count_ref[...] += dot_t(hot_dst, hot_src)
        return carry

    lax.fori_loop(0, dst_ref.shape[0] // group, step, 0)


def attend_kernel(
    x_ref, far_ref, gain_ref, wq_ref, wk_ref, wv_ref, wo_ref, cot_ref,
    q_ref, k_ref, v_ref, qt_ref, normt_ref, datt_ref, count_ref,
    out_ref, gf_ref, pay_ref, w_scr, g_scr, dkt_scr, dvt_scr,
):
    rows, feats = x_ref.shape
    far = far_ref.shape[0]
    width = count_ref.shape[1]
    head = feats // HEADS
    peers, block, _ = pay_ref.shape
    slots = far // peers
    pad = width - rows - far
    far_x = far_ref[...].astype(F32)
    if pad:
        far_x = jnp.concatenate([far_x, jnp.zeros((pad, feats), F32)], axis=0)
    x = x_ref[...].astype(F32)
    gain = gain_ref[...]
    far_hat, far_rstd = standardize(far_x)
    far_normed = (far_hat * gain).astype(BF16)
    keys = jnp.concatenate([k_ref[...], dot(far_normed, wk_ref[...]).astype(BF16)], axis=0)
    values = jnp.concatenate([v_ref[...], dot(far_normed, wv_ref[...]).astype(BF16)], axis=0)
    lane = lax.broadcasted_iota(jnp.int32, (1, feats), 1)
    masks = [(lane >= h * head) & (lane < (h + 1) * head) for h in range(HEADS)]
    hots = [m.astype(F32).astype(BF16) for m in masks]
    queries = q_ref[...]
    count = count_ref[...]
    num = jnp.zeros((rows, feats), F32)
    den = jnp.zeros((rows, feats), F32)
    for h in range(HEADS):
        score = dot_t(queries * hots[h], keys)
        t = jnp.tanh(score * (0.2 / math.sqrt(head)))
        w = count * jnp.exp(5.0 * t)
        wb = w.astype(BF16)
        w_scr[h] = wb
        g_scr[h] = w * (1.0 - t * t) * (1.0 / math.sqrt(head))
        num = num + dot(wb, values * hots[h])
        den = den + dot(wb, jnp.broadcast_to(hots[h], (width, feats)))
    rden = 1.0 / den
    att32 = num * rden
    att = att32.astype(BF16)
    out_ref[...] = (x + dot(att, wo_ref[...])).astype(BF16)
    grad_out = dot(att.T, cot_ref[...])
    dnum = (datt_ref[...].astype(F32) * rden).astype(BF16)
    dnum_t = dnum.T
    prod = dnum.astype(F32) * att32
    qt = qt_ref[...]
    dq = jnp.zeros((rows, feats), F32)
    for h in range(HEADS):
        z = jnp.sum(jnp.where(masks[h], prod, 0.0), axis=1, keepdims=True)
        ds = (g_scr[h] * (dot_t(dnum * hots[h], values) - z)).astype(BF16)
        dq = dq + dot(ds, keys * hots[h])
        at = slice(h * head, (h + 1) * head)
        dkt_scr[at, :] = dot(qt[at, :], ds)
        dvt_scr[at, :] = dot(dnum_t[at, :], w_scr[h])
    dq = dq.astype(BF16)
    dkt = dkt_scr[...].astype(BF16)
    dvt = dvt_scr[...].astype(BF16)
    norm_t = jnp.concatenate([normt_ref[...], far_normed.T], axis=1)
    grad_query = dot(normt_ref[...], dq)
    grad_key = dot_t(norm_t, dkt)
    grad_value = dot_t(norm_t, dvt)
    d_normed = (dot(wk_ref[...], dkt) + dot(wv_ref[...], dvt)).T
    near = d_normed[:rows] + dot_t(dq, wq_ref[...])
    away = d_normed[rows:]
    hat, rstd = standardize(x)

    def pull(d, xhat, scale):
        g = d * gain
        mean_g = jnp.mean(g, axis=1, keepdims=True)
        mean_gx = jnp.mean(g * xhat, axis=1, keepdims=True)
        return scale * (g - mean_g - xhat * mean_gx)

    gf_ref[...] = cot_ref[...].astype(F32) + pull(near, hat, rstd)
    away_dx = pull(away, far_hat, far_rstd)
    gain_sum = jnp.sum(near * hat, axis=0, keepdims=True) + jnp.sum(
        away * far_hat, axis=0, keepdims=True
    )
    grads = jnp.concatenate([grad_query, grad_key, grad_value, grad_out], axis=0)
    share = grads.shape[0] // peers
    blank = jnp.zeros((block - share - slots - 1, feats), F32)
    for p in range(peers):
        pay_ref[p] = jnp.concatenate(
            [
                grads[p * share : (p + 1) * share],
                away_dx[p * slots : (p + 1) * slots],
                gain_sum,
                blank,
            ],
            axis=0,
        ).astype(BF16)


def reduce_kernel(got_ref, share_ref):
    peers, share, _ = share_ref.shape
    total = jnp.zeros(share_ref.shape[1:], F32)
    for p in range(peers):
        total = total + got_ref[p].astype(F32)[:share]
    share_ref[...] = jnp.broadcast_to(total.astype(BF16)[None], share_ref.shape)


def finish_kernel(share, send_ref, gf_ref, got_ref, feats_ref, gain_ref):
    peers, slots = send_ref.shape
    feats_ref[...] = gf_ref[...]
    gain = jnp.zeros(gain_ref.shape, F32)
    for p in range(peers):
        got = got_ref[p].astype(F32)
        gain = gain + got[share + slots : share + slots + 1]
        for slot in range(slots):
            at = pl.ds(send_ref[p, slot], 1)
            feats_ref[at, :] += got[share + slot : share + slot + 1]
    gain_ref[...] = gain


def spread_kernel(got_ref, *out_refs):
    rows = out_refs[0].shape[0]
    peers, share, feats = got_ref.shape
    whole = got_ref[...].astype(F32).reshape(peers * share, feats)
    for i, out_ref in enumerate(out_refs):
        out_ref[...] = whole[i * rows : (i + 1) * rows]


def call(kernel, out_shape, n_in, scratch=(), smem=(), cost=None):
    return pl.pallas_call(
        kernel,
        out_shape=out_shape,
        in_specs=[SMEM if i in smem else VMEM for i in range(n_in)],
        out_specs=jax.tree.map(lambda _: VMEM, out_shape),
        scratch_shapes=list(scratch),
        compiler_params=pltpu.CompilerParams(vmem_limit_bytes=LIMIT),
        cost_estimate=cost,
    )


def on_device(
    node_feats, norm_gain, w_query, w_key, w_value, w_out, cotangent,
    edge_dst, edge_src, edge_mask, send_rows,
):
    rows, feats = node_feats.shape
    peers, slots = send_rows.shape[1:]
    far = peers * slots
    width = rows + up(far, 128)
    share = 4 * feats // peers
    block = up(share + slots + 1, 16)
    gain = norm_gain.reshape(1, feats)
    send = send_rows[0]

    def like(shape, dtype):
        return jax.ShapeDtypeStruct(shape, dtype)

    picked = call(
        pick_kernel,
        like((far, feats), BF16),
        2,
        (pltpu.VMEM((rows, feats), F32), pltpu.VMEM((far, feats), F32)),
        smem=(0,),
    )(send, node_feats)
    arrived = lax.all_to_all(
        picked.reshape(peers, slots, feats), "nodes", split_axis=0, concat_axis=0, tiled=True
    ).reshape(far, feats)
    square = like((rows, feats), BF16)
    cost = pl.CostEstimate(flops=2_000_000_000, bytes_accessed=2_000_000, transcendentals=0)
    near = call(
        local_kernel,
        (square, square, square, like((feats, rows), BF16), like((feats, rows), BF16), square,
         like((rows, width), F32)),
        10,
        cost=cost,
    )(node_feats, gain, w_query, w_key, w_value, w_out, cotangent, edge_dst, edge_src, edge_mask)
    output, gf, payload = call(
        attend_kernel,
        (square, like((rows, feats), F32), like((peers, block, feats), BF16)),
        15,
        (
            pltpu.VMEM((HEADS, rows, width), BF16),
            pltpu.VMEM((HEADS, rows, width), F32),
            pltpu.VMEM((feats, width), F32),
            pltpu.VMEM((feats, width), F32),
        ),
    )(node_feats, arrived, gain, w_query, w_key, w_value, w_out, cotangent, *near)
    got = lax.all_to_all(payload, "nodes", split_axis=0, concat_axis=0, tiled=True)
    shares = call(reduce_kernel, like((peers, share, feats), BF16), 1)(got)
    whole = lax.all_to_all(shares, "nodes", split_axis=0, concat_axis=0, tiled=True)
    grad_feats, grad_gain = call(
        functools.partial(finish_kernel, share),
        (like((rows, feats), F32), like((1, feats), F32)),
        3,
        smem=(0,),
    )(send, gf, got)
    grads = call(spread_kernel, (like((feats, feats), F32),) * 4, 1)(whole)
    return (output, grad_feats, grad_gain.reshape(feats), *grads)


def solution(mesh):
    nodes = P(("groups", "nodes"), None)
    in_specs = (
        nodes, P(), P(), P(), P(), P(), nodes, nodes, nodes, nodes,
        P(("groups", "nodes"), None, None),
    )
    out_specs = (nodes, nodes, P("groups")) + (P("groups", None),) * 4
    return jax.shard_map(
        on_device, mesh=mesh, in_specs=in_specs, out_specs=out_specs, check_vma=False
    )
```

```python
import functools
import math

import jax
import jax.numpy as jnp
from jax import lax
from jax.experimental import pallas as pl
from jax.experimental.pallas import tpu as pltpu
from jax.sharding import PartitionSpec as P

HEADS = 8
EPS = 1e-05
F32 = jnp.float32
BF16 = jnp.bfloat16
VMEM = pl.BlockSpec(memory_space=pltpu.VMEM)
SMEM = pl.BlockSpec(memory_space=pltpu.SMEM)
ANY = pl.BlockSpec(memory_space=pl.ANY)
LIMIT = 40 * 1024 * 1024


def up(n, m):
    return -(-n // m) * m


def dot(a, b):
    return jnp.dot(a, b, preferred_element_type=F32)


def dot_t(a, b):
    return lax.dot_general(a, b, (((1,), (1,)), ((), ())), preferred_element_type=F32)


def standardize(x):
    centered = x - jnp.mean(x, axis=1, keepdims=True)
    rstd = lax.rsqrt(jnp.mean(centered * centered, axis=1, keepdims=True) + EPS)
    return centered * rstd, rstd


def pick_kernel(send_ref, feats_hbm, out_ref, feats, wide, sem):
    slots, peers = send_ref.shape
    copy = pltpu.make_async_copy(feats_hbm, feats, sem)
    copy.start()
    copy.wait()
    wide[...] = feats[...].astype(F32)
    for peer in range(peers):
        rows = [wide[pl.ds(send_ref[slot, peer], 1), :] for slot in range(slots)]
        out_ref[peer] = jnp.concatenate(rows, axis=0).astype(BF16)


def local_kernel(*refs):
    n = 10
    fetched = refs[n + 7 : n + 7 + n]
    sems = refs[-1]
    copies = [
        pltpu.make_async_copy(refs[i], fetched[i], sems.at[i]) for i in range(n)
    ]
    for copy in copies:
        copy.start()
    for copy in copies:
        copy.wait()
    local_body(*fetched, *refs[n : n + 7])


def local_body(
    x_ref, gain_ref, wq_ref, wk_ref, wv_ref, wo_ref, cot_ref, dst_ref, src_ref, mask_ref,
    q_ref, k_ref, v_ref, qt_ref, normt_ref, datt_ref, count_ref,
):
    rows = x_ref.shape[0]
    width = count_ref.shape[1]
    xhat, _ = standardize(x_ref[...].astype(F32))
    normed = (xhat * gain_ref[...]).astype(BF16)
    q = dot(normed, wq_ref[...]).astype(BF16)
    q_ref[...] = q
    qt_ref[...] = q.T
    normt_ref[...] = normed.T
    k_ref[...] = dot(normed, wk_ref[...]).astype(BF16)
    v_ref[...] = dot(normed, wv_ref[...]).astype(BF16)
    datt_ref[...] = dot_t(cot_ref[...], wo_ref[...]).astype(BF16)
    row_id = lax.broadcasted_iota(jnp.int32, (rows, width), 0)
    col_id = lax.broadcasted_iota(jnp.int32, (rows, width), 1)
    count_ref[...] = (row_id == col_id).astype(F32)
    group = 8
    edge = 128
    dst_id = lax.broadcasted_iota(jnp.int32, (rows, edge), 0)
    src_id = lax.broadcasted_iota(jnp.int32, (width, edge), 0)

    def step(i, carry):
        base = pl.multiple_of(i * group, group)
        dst = dst_ref[pl.ds(base, group), :]
        src = jnp.where(mask_ref[pl.ds(base, group), :] > 0, src_ref[pl.ds(base, group), :], -1)
        hot_dst = jnp.concatenate(
            [(dst_id == dst[j : j + 1]).astype(F32).astype(BF16) for j in range(group)], axis=1
        )
        hot_src = jnp.concatenate(
            [(src_id == src[j : j + 1]).astype(F32).astype(BF16) for j in range(group)], axis=1
        )
        count_ref[...] += dot_t(hot_dst, hot_src)
        return carry

    lax.fori_loop(0, dst_ref.shape[0] // group, step, 0)


def attend_kernel(
    x_ref, far_ref, gain_ref, wq_ref, wk_ref, wv_ref, wo_ref, cot_ref,
    q_ref, k_ref, v_ref, qt_ref, normt_ref, datt_ref, count_ref,
    out_ref, gf_ref, keep_ref, give_ref, w_scr, g_scr, dkt_scr, dvt_scr, grad_scr, away_scr,
):
    rows, feats = x_ref.shape
    peers, slots, _ = far_ref.shape
    far = peers * slots
    width = count_ref.shape[1]
    head = feats // HEADS
    chips, block, _ = keep_ref.shape
    pad = width - rows - far
    far_x = jnp.concatenate([far_ref[p].astype(F32) for p in range(peers)], axis=0)
    if pad:
        far_x = jnp.concatenate([far_x, jnp.zeros((pad, feats), F32)], axis=0)
    x = x_ref[...].astype(F32)
    gain = gain_ref[...]
    far_hat, far_rstd = standardize(far_x)
    far_normed = (far_hat * gain).astype(BF16)
    keys = jnp.concatenate([k_ref[...], dot(far_normed, wk_ref[...]).astype(BF16)], axis=0)
    values = jnp.concatenate([v_ref[...], dot(far_normed, wv_ref[...]).astype(BF16)], axis=0)
    lane = lax.broadcasted_iota(jnp.int32, (1, feats), 1)
    masks = [(lane >= h * head) & (lane < (h + 1) * head) for h in range(HEADS)]
    hots = [m.astype(F32).astype(BF16) for m in masks]
    queries = q_ref[...]
    count = count_ref[...]
    num = jnp.zeros((rows, feats), F32)
    den = jnp.zeros((rows, feats), F32)
    for h in range(HEADS):
        score = dot_t(queries * hots[h], keys)
        t = jnp.tanh(score * (0.2 / math.sqrt(head)))
        w = count * jnp.exp(5.0 * t)
        wb = w.astype(BF16)
        w_scr[h] = wb
        g_scr[h] = w * (1.0 - t * t) * (1.0 / math.sqrt(head))
        num = num + dot(wb, values * hots[h])
        den = den + dot(wb, jnp.broadcast_to(hots[h], (width, feats)))
    rden = 1.0 / den
    att32 = num * rden
    att = att32.astype(BF16)
    out_ref[...] = (x + dot(att, wo_ref[...])).astype(BF16)
    grad_out = dot(att.T, cot_ref[...])
    dnum = (datt_ref[...].astype(F32) * rden).astype(BF16)
    dnum_t = dnum.T
    prod = dnum.astype(F32) * att32
    qt = qt_ref[...]
    dq = jnp.zeros((rows, feats), F32)
    for h in range(HEADS):
        z = jnp.sum(jnp.where(masks[h], prod, 0.0), axis=1, keepdims=True)
        ds = (g_scr[h] * (dot_t(dnum * hots[h], values) - z)).astype(BF16)
        dq = dq + dot(ds, keys * hots[h])
        at = slice(h * head, (h + 1) * head)
        dkt_scr[at, :] = dot(qt[at, :], ds)
        dvt_scr[at, :] = dot(dnum_t[at, :], w_scr[h])
    dq = dq.astype(BF16)
    dkt = dkt_scr[...].astype(BF16)
    dvt = dvt_scr[...].astype(BF16)
    norm_t = jnp.concatenate([normt_ref[...], far_normed.T], axis=1)
    grad_query = dot(normt_ref[...], dq)
    grad_key = dot_t(norm_t, dkt)
    grad_value = dot_t(norm_t, dvt)
    d_normed = (dot(wk_ref[...], dkt) + dot(wv_ref[...], dvt)).T
    near = d_normed[:rows] + dot_t(dq, wq_ref[...])
    away = d_normed[rows:]
    hat, rstd = standardize(x)

    def pull(d, xhat, scale):
        g = d * gain
        mean_g = jnp.mean(g, axis=1, keepdims=True)
        mean_gx = jnp.mean(g * xhat, axis=1, keepdims=True)
        return scale * (g - mean_g - xhat * mean_gx)

    gf_ref[...] = cot_ref[...].astype(F32) + pull(near, hat, rstd)
    away_dx = pull(away, far_hat, far_rstd)
    gain_sum = jnp.sum(near * hat, axis=0, keepdims=True) + jnp.sum(
        away * far_hat, axis=0, keepdims=True
    )
    grad_scr[...] = jnp.concatenate([grad_query, grad_key, grad_value, grad_out], axis=0)
    away_scr[...] = away_dx
    half = grad_scr.shape[0] // 2
    share = half // chips
    blank = jnp.zeros((block - share - slots - 1, feats), F32)
    core = lax.rem(lax.axis_index("nodes"), 2)
    for c in range(chips):
        for own in (True, False):
            which = core if own else 1 - core
            start = pl.multiple_of(which * half + c * share, 8)
            dx = [away_dx[(2 * c + i) * slots : (2 * c + i + 1) * slots] for i in range(2)]
            part = jnp.concatenate(
                [
                    grad_scr[pl.ds(start, share), :],
                    jnp.where(which == 0, dx[0], dx[1]),
                    gain_sum,
                    blank,
                ],
                axis=0,
            )
            if own:
                keep_ref[c] = part
            else:
                give_ref[c] = part.astype(BF16)


def pair_kernel(share, slots, keep_ref, got_ref, out_ref):
    chips, block, feats = out_ref.shape
    blank = jnp.zeros((block - share - 2 * slots - 1, feats), F32)
    for c in range(chips):
        keep = keep_ref[c]
        got = got_ref[c].astype(F32)
        out_ref[c] = jnp.concatenate(
            [
                keep[:share] + got[:share],
                keep[share : share + slots],
                got[share : share + slots],
                keep[share + slots : share + slots + 1] + got[share + slots : share + slots + 1],
                blank,
            ],
            axis=0,
        ).astype(BF16)


def reduce_kernel(got_ref, share_ref):
    chips, share, _ = share_ref.shape
    total = jnp.zeros(share_ref.shape[1:], F32)
    for c in range(chips):
        total = total + got_ref[c].astype(F32)[:share]
    share_ref[...] = jnp.broadcast_to(total.astype(BF16)[None], share_ref.shape)


def finish_kernel(share, send_ref, gf_ref, got_ref, feats_ref, gain_ref):
    slots, peers = send_ref.shape
    feats_ref[...] = gf_ref[...]
    gain = jnp.zeros(gain_ref.shape, F32)
    core = lax.rem(lax.axis_index("nodes"), 2)
    for c in range(peers // 2):
        got = got_ref[c].astype(F32)
        gain = gain + got[share + 2 * slots : share + 2 * slots + 1]
        for i in range(2 * slots):
            peer = 2 * c + (core if i < slots else 1 - core)
            at = pl.ds(send_ref[i % slots, peer], 1)
            feats_ref[at, :] += got[share + i : share + i + 1]
    gain_ref[...] = gain


def spread_kernel(mine_ref, other_ref, *out_refs):
    rows = out_refs[0].shape[0]
    chips, share, feats = mine_ref.shape
    first = lax.rem(lax.axis_index("nodes"), 2) == 0
    mine = mine_ref[...].astype(F32).reshape(chips * share, feats)
    other = other_ref[...].astype(F32).reshape(chips * share, feats)
    low = jnp.where(first, mine, other)
    high = jnp.where(first, other, mine)
    out_refs[0][...] = low[:rows]
    out_refs[1][...] = low[rows:]
    out_refs[2][...] = high[:rows]
    out_refs[3][...] = high[rows:]


def call(kernel, out_shape, n_in, scratch=(), smem=(), hbm=(), cost=None):
    return pl.pallas_call(
        kernel,
        out_shape=out_shape,
        in_specs=[SMEM if i in smem else ANY if i in hbm else VMEM for i in range(n_in)],
        out_specs=jax.tree.map(lambda _: VMEM, out_shape),
        scratch_shapes=list(scratch),
        compiler_params=pltpu.CompilerParams(vmem_limit_bytes=LIMIT),
        cost_estimate=cost,
    )


def on_device(
    node_feats, norm_gain, w_query, w_key, w_value, w_out, cotangent,
    edge_dst, edge_src, edge_mask, send_rows,
):
    rows, feats = node_feats.shape
    peers, slots = send_rows.shape[1:]
    far = peers * slots
    width = rows + up(far, 128)
    chips = peers // 2
    share = 2 * feats // chips
    block = up(share + slots + 1, 16)
    message = up(share + 2 * slots + 1, 16)
    gain = norm_gain.reshape(1, feats)
    send = send_rows[0].T
    swap = [(i, i ^ 1) for i in range(peers)]
    sides = [list(range(k, peers, 2)) for k in range(2)]

    def like(shape, dtype):
        return jax.ShapeDtypeStruct(shape, dtype)

    def across(x):
        return lax.all_to_all(x, "nodes", 0, 0, axis_index_groups=sides, tiled=True)

    picked = call(
        pick_kernel,
        like((peers, slots, feats), BF16),
        2,
        (pltpu.VMEM((rows, feats), BF16), pltpu.VMEM((rows, feats), F32),
         pltpu.SemaphoreType.DMA),
        smem=(0,),
        hbm=(1,),
    )(send, node_feats)
    arrived = lax.all_to_all(picked, "nodes", split_axis=0, concat_axis=0, tiled=True)
    square = like((rows, feats), BF16)
    cost = pl.CostEstimate(flops=2_000_000_000, bytes_accessed=2_000_000, transcendentals=0)
    operands = (
        node_feats, gain, w_query, w_key, w_value, w_out, cotangent, edge_dst, edge_src, edge_mask
    )
    near = call(
        local_kernel,
        (square, square, square, like((feats, rows), BF16), like((feats, rows), BF16), square,
         like((rows, width), F32)),
        10,
        [pltpu.VMEM(a.shape, a.dtype) for a in operands] + [pltpu.SemaphoreType.DMA((10,))],
        hbm=range(10),
        cost=cost,
    )(*operands)
    output, gf, keep, give = call(
        attend_kernel,
        (square, like((rows, feats), F32), like((chips, block, feats), F32),
         like((chips, block, feats), BF16)),
        15,
        (
            pltpu.VMEM((HEADS, rows, width), BF16),
            pltpu.VMEM((HEADS, rows, width), F32),
            pltpu.VMEM((feats, width), F32),
            pltpu.VMEM((feats, width), F32),
            pltpu.VMEM((4 * feats, feats), F32),
            pltpu.VMEM((width - rows, feats), F32),
        ),
    )(node_feats, arrived, gain, w_query, w_key, w_value, w_out, cotangent, *near)
    given = lax.ppermute(give, "nodes", swap)
    paired = call(
        functools.partial(pair_kernel, share, slots), like((chips, message, feats), BF16), 2
    )(keep, given)
    got = across(paired)
    shares = call(reduce_kernel, like((chips, share, feats), BF16), 1)(got)
    mine = across(shares)
    other = lax.ppermute(mine, "nodes", swap)
    grad_feats, grad_gain = call(
        functools.partial(finish_kernel, share),
        (like((rows, feats), F32), like((1, feats), F32)),
        3,
        smem=(0,),
    )(send, gf, got)
    grads = call(spread_kernel, (like((feats, feats), F32),) * 4, 2)(mine, other)
    return (output, grad_feats, grad_gain.reshape(feats), *grads)


def solution(mesh):
    nodes = P(("groups", "nodes"), None)
    in_specs = (
        nodes, P(), P(), P(), P(), P(), nodes, nodes, nodes, nodes,
        P(("groups", "nodes"), None, None),
    )
    out_specs = (nodes, nodes, P("groups")) + (P("groups", None),) * 4
    return jax.shard_map(
        on_device, mesh=mesh, in_specs=in_specs, out_specs=out_specs, check_vma=False
    )
```

```python
import functools
import math

import jax
import jax.numpy as jnp
from jax import lax
from jax.experimental import pallas as pl
from jax.experimental.pallas import tpu as pltpu
from jax.sharding import PartitionSpec as P

HEADS = 8
EARLY = 4
EPS = 1e-05
F32 = jnp.float32
BF16 = jnp.bfloat16
VMEM = pl.BlockSpec(memory_space=pltpu.VMEM)
SMEM = pl.BlockSpec(memory_space=pltpu.SMEM)
HBM = pl.BlockSpec(memory_space=pltpu.HBM)
MIB = 1024 * 1024
FULL = 60


def up(n, m):
    return -(-n // m) * m


def dot(a, b):
    return jnp.dot(a, b, preferred_element_type=F32)


def dot_t(a, b):
    return lax.dot_general(a, b, (((1,), (1,)), ((), ())), preferred_element_type=F32)


def standardize(x):
    centered = x - jnp.mean(x, axis=1, keepdims=True)
    rstd = lax.rsqrt(jnp.mean(centered * centered, axis=1, keepdims=True) + EPS)
    return centered * rstd, rstd


def pull(g, xhat, rstd):
    mean_g = jnp.mean(g, axis=1, keepdims=True)
    mean_gx = jnp.mean(g * xhat, axis=1, keepdims=True)
    return rstd * (g - mean_g - xhat * mean_gx)


def begin(sources, targets, sems):
    copies = [
        pltpu.make_async_copy(source, target, sems.at[i])
        for i, (source, target) in enumerate(zip(sources, targets))
    ]
    for copy in copies:
        copy.start()
    return copies


def finish_all(copies):
    for copy in copies:
        copy.wait()


def pick_kernel(send_hbm, *refs):
    squares = refs[:6]
    edges = refs[6:9]
    out_ref, square_ref, edge_ref, send, wide, sems = refs[9:]
    copies = begin(
        (send_hbm,) + squares + edges,
        [send] + [square_ref.at[i] for i in range(6)] + [edge_ref.at[i] for i in range(3)],
        sems,
    )
    finish_all(copies[:2])
    slots, peers = send.shape
    wide[...] = square_ref[0].astype(F32)
    for peer in range(peers):
        rows = [wide[pl.ds(send[slot, peer], 1), :] for slot in range(slots)]
        out_ref[peer] = jnp.concatenate(rows, axis=0).astype(BF16)
    finish_all(copies[2:])


def head_hots(feats):
    lane = lax.broadcasted_iota(jnp.int32, (1, feats), 1)
    size = feats // HEADS
    masks = [(lane >= h * size) & (lane < (h + 1) * size) for h in range(HEADS)]
    return masks, [m.astype(F32).astype(BF16) for m in masks]


def weigh(queries, keys, count, head):
    t = jnp.tanh(dot_t(queries, keys) * (0.2 / math.sqrt(head)))
    w = count * jnp.exp(5.0 * t)
    return w.astype(BF16), (w * (1.0 - t * t) * (1.0 / math.sqrt(head))).astype(BF16)


def local_kernel(gain_ref, square_ref, edge_ref, low_ref, far_count, near_count, w_ref, g_ref):
    x_ref, wq_ref, wk_ref, wv_ref, wo_ref, cot_ref = [square_ref.at[i] for i in range(6)]
    queries, keys = local_project(
        x_ref, gain_ref, wq_ref, wk_ref, wv_ref, wo_ref, cot_ref, low_ref
    )
    rows, feats = queries.shape
    local_count(edge_ref.at[0], edge_ref.at[1], edge_ref.at[2], far_count, near_count)
    _, hots = head_hots(feats)
    for h in range(EARLY):
        w_ref[h], g_ref[h] = weigh(queries * hots[h], keys, near_count[...], feats // HEADS)


def local_project(x_ref, gain_ref, wq_ref, wk_ref, wv_ref, wo_ref, cot_ref, low_ref):
    xhat, _ = standardize(x_ref[...].astype(F32))
    normed = (xhat * gain_ref[...]).astype(BF16)
    queries = dot(normed, wq_ref[...]).astype(BF16)
    keys = dot(normed, wk_ref[...]).astype(BF16)
    low_ref[0] = queries
    low_ref[1] = keys
    low_ref[2] = dot(normed, wv_ref[...]).astype(BF16)
    low_ref[3] = queries.T
    low_ref[4] = normed.T
    low_ref[5] = dot_t(cot_ref[...], wo_ref[...]).astype(BF16)
    return queries, keys


def local_count(dst_ref, src_ref, mask_ref, far_count, near_count):
    rows, far = far_count.shape
    row_id = lax.broadcasted_iota(jnp.int32, (rows, rows), 0)
    col_id = lax.broadcasted_iota(jnp.int32, (rows, rows), 1)
    near_count[...] = (row_id == col_id).astype(F32)
    far_count[...] = jnp.zeros((rows, far), F32)
    group = 8
    edge = 128
    dst_id = lax.broadcasted_iota(jnp.int32, (rows, edge), 0)
    src_id = lax.broadcasted_iota(jnp.int32, (rows + far, edge), 0)

    def step(i, carry):
        base = pl.multiple_of(i * group, group)
        dst = dst_ref[pl.ds(base, group), :]
        src = jnp.where(mask_ref[pl.ds(base, group), :] > 0, src_ref[pl.ds(base, group), :], -1)
        hot_dst = jnp.concatenate(
            [(dst_id == dst[j : j + 1]).astype(F32).astype(BF16) for j in range(group)], axis=1
        )
        hot_src = jnp.concatenate(
            [(src_id == src[j : j + 1]).astype(F32).astype(BF16) for j in range(group)], axis=1
        )
        part = dot_t(hot_dst, hot_src)
        near_count[...] += part[:, :rows]
        far_count[...] += part[:, rows:]
        return carry

    lax.fori_loop(0, dst_ref.shape[0] // group, step, 0)


def attend_kernel(
    far_ref, gain_ref, square_ref, low_ref, far_count, near_count, near_w, near_g,
    att_ref, near_ref, keep_ref, give_ref,
    w_scr, g_scr, dkt_scr, dvt_scr, grad_scr,
):
    _, wq_ref, wk_ref, wv_ref, _, cot_ref = [square_ref.at[i] for i in range(6)]
    _, rows, feats = low_ref.shape
    q_ref, k_ref, v_ref, qt_ref, normt_ref, datt_ref = [low_ref.at[i] for i in range(6)]
    peers, slots, _ = far_ref.shape
    far = peers * slots
    width = far_count.shape[1]
    head = feats // HEADS
    chips, block, _ = keep_ref.shape
    pad = width - far
    far_x = jnp.concatenate([far_ref[p].astype(F32) for p in range(peers)], axis=0)
    if pad:
        far_x = jnp.concatenate([far_x, jnp.zeros((pad, feats), F32)], axis=0)
    gain = gain_ref[...]
    far_hat, far_rstd = standardize(far_x)
    far_normed = (far_hat * gain).astype(BF16)
    far_keys = dot(far_normed, wk_ref[...]).astype(BF16)
    far_values = dot(far_normed, wv_ref[...]).astype(BF16)
    keys = jnp.concatenate([k_ref[...], far_keys], axis=0)
    values = jnp.concatenate([v_ref[...], far_values], axis=0)
    masks, hots = head_hots(feats)
    queries = q_ref[...]
    count = far_count[...]
    both_count = jnp.concatenate([near_count[...], count], axis=1)
    num = jnp.zeros((rows, feats), F32)
    den = jnp.zeros((rows, feats), F32)
    for h in range(HEADS):
        q_head = queries * hots[h]
        if h < EARLY:
            w, g = weigh(q_head, far_keys, count, head)
            w = jnp.concatenate([near_w[h], w], axis=1)
            g = jnp.concatenate([near_g[h], g], axis=1)
        else:
            w, g = weigh(q_head, keys, both_count, head)
        w_scr[h] = w
        g_scr[h] = g
        num = num + dot(w, values * hots[h])
        den = den + dot(w, jnp.broadcast_to(hots[h], (rows + width, feats)))
    rden = 1.0 / den
    att32 = num * rden
    att = att32.astype(BF16)
    att_ref[...] = att
    grad_out = dot(att.T, cot_ref[...])
    dnum = (datt_ref[...].astype(F32) * rden).astype(BF16)
    dnum_t = dnum.T
    prod = dnum.astype(F32) * att32
    qt = qt_ref[...]
    dq = jnp.zeros((rows, feats), F32)
    for h in range(HEADS):
        z = jnp.sum(jnp.where(masks[h], prod, 0.0), axis=1, keepdims=True)
        dw = dot_t(dnum * hots[h], values) - z
        ds = (g_scr[h].astype(F32) * dw).astype(BF16)
        dq = dq + dot(ds, keys * hots[h])
        at = slice(h * head, (h + 1) * head)
        dkt_scr[at, :] = dot(qt[at, :], ds)
        dvt_scr[at, :] = dot(dnum_t[at, :], w_scr[h])
    dq = dq.astype(BF16)
    dkt = dkt_scr[...].astype(BF16)
    dvt = dvt_scr[...].astype(BF16)
    norm_t = jnp.concatenate([normt_ref[...], far_normed.T], axis=1)
    grad_query = dot(normt_ref[...], dq)
    grad_key = dot_t(norm_t, dkt)
    grad_value = dot_t(norm_t, dvt)
    d_normed = (dot(wk_ref[...], dkt) + dot(wv_ref[...], dvt)).T
    near = d_normed[:rows] + dot_t(dq, wq_ref[...])
    near_ref[...] = near
    away = d_normed[rows:]
    away_dx = pull(away * gain, far_hat, far_rstd)
    grad_scr[...] = jnp.concatenate([grad_query, grad_key, grad_value, grad_out], axis=0)
    half = grad_scr.shape[0] // 2
    share = half // chips
    blank = jnp.zeros((block - share - slots, feats), F32)
    core = lax.rem(lax.axis_index("nodes"), 2)
    for c in range(chips):
        for own in (True, False):
            which = core if own else 1 - core
            start = pl.multiple_of(which * half + c * share, 8)
            dx = [away_dx[(2 * c + i) * slots : (2 * c + i + 1) * slots] for i in range(2)]
            part = jnp.concatenate(
                [grad_scr[pl.ds(start, share), :], jnp.where(which == 0, dx[0], dx[1]), blank],
                axis=0,
            )
            if own:
                keep_ref[c] = part
            else:
                give_ref[c] = part.astype(BF16)


def pair_kernel(share, slots, keep_ref, got_ref, out_ref):
    chips, block, feats = out_ref.shape
    blank = [jnp.zeros((block - share - 2 * slots, feats), F32)] * (block > share + 2 * slots)
    for c in range(chips):
        keep = keep_ref[c]
        got = got_ref[c].astype(F32)
        end = share + slots
        out_ref[c] = jnp.concatenate(
            [keep[:share] + got[:share], keep[share:end], got[share:end]] + blank, axis=0
        ).astype(BF16)


def reduce_kernel(got_ref, share_ref):
    chips, share, _ = share_ref.shape
    total = jnp.zeros(share_ref.shape[1:], F32)
    for c in range(chips):
        total = total + got_ref[c].astype(F32)[:share]
    share_ref[...] = jnp.broadcast_to(total.astype(BF16)[None], share_ref.shape)


def own_kernel(square_ref, gain_ref, near_ref, att_ref, out_ref, feats_ref):
    x = square_ref[0].astype(F32)
    out_ref[...] = (x + dot(att_ref[...], square_ref[4])).astype(BF16)
    dx = pull(near_ref[...] * gain_ref[...], *standardize(x))
    feats_ref[...] = square_ref[5].astype(F32) + dx


def finish_kernel(share, send_ref, got_ref, own_ref, feats_ref):
    slots, peers = send_ref.shape
    feats_ref[...] = own_ref[...]
    core = lax.rem(lax.axis_index("nodes"), 2)
    for c in range(peers // 2):
        got = got_ref[c].astype(F32)
        for i in range(2 * slots):
            peer = 2 * c + (core if i < slots else 1 - core)
            at = pl.ds(send_ref[i % slots, peer], 1)
            feats_ref[at, :] += got[share + i : share + i + 1]


def spread_kernel(mine_ref, other_ref, gain_ref, wq_ref, wk_ref, wv_ref, *out_refs):
    rows = wq_ref.shape[0]
    chips, share, feats = mine_ref.shape
    first = lax.rem(lax.axis_index("nodes"), 2) == 0
    mine = mine_ref[...].astype(F32).reshape(chips * share, feats)
    other = other_ref[...].astype(F32).reshape(chips * share, feats)
    low = jnp.where(first, mine, other)
    high = jnp.where(first, other, mine)
    grads = (low[:rows], low[rows:], high[:rows], high[rows:])
    for grad, out_ref in zip(grads, out_refs):
        out_ref[...] = grad
    prod = jnp.zeros((rows, feats), F32)
    for grad, w_ref in zip(grads, (wq_ref, wk_ref, wv_ref)):
        prod = prod + grad * w_ref[...].astype(F32)
    out_refs[4][...] = jnp.sum(prod.T, axis=0, keepdims=True) / gain_ref[...]


def call(kernel, out_shape, in_specs, scratch=(), cost=None, out_specs=None, mib=16):
    return pl.pallas_call(
        kernel,
        out_shape=out_shape,
        in_specs=in_specs,
        out_specs=jax.tree.map(lambda _: VMEM, out_shape) if out_specs is None else out_specs,
        scratch_shapes=list(scratch),
        compiler_params=pltpu.CompilerParams(vmem_limit_bytes=mib * MIB),
        cost_estimate=cost,
    )


def on_device(
    node_feats, norm_gain, w_query, w_key, w_value, w_out, cotangent,
    edge_dst, edge_src, edge_mask, send_rows,
):
    rows, feats = node_feats.shape
    peers, slots = send_rows.shape[1:]
    far = peers * slots
    width = up(far, 128)
    chips = peers // 2
    share = 2 * feats // chips
    block = up(share + slots, 8)
    message = up(share + 2 * slots, 8)
    gain = norm_gain.reshape(1, feats)
    send = send_rows[0].T
    swap = [(i, i ^ 1) for i in range(peers)]
    sides = [list(range(k, peers, 2)) for k in range(2)]

    def like(shape, dtype):
        return jax.ShapeDtypeStruct(shape, dtype)

    def across(x):
        return lax.all_to_all(x, "nodes", 0, 0, axis_index_groups=sides, tiled=True)

    cost = pl.CostEstimate(flops=8_000_000_000, bytes_accessed=2_000_000, transcendentals=0)
    square = like((rows, feats), BF16)
    wide = like((rows, feats), F32)
    picked, squares, edges = call(
        pick_kernel,
        (like((peers, slots, feats), BF16), like((6, rows, feats), BF16),
         like((3,) + edge_dst.shape, jnp.int32)),
        [HBM] * 10,
        (pltpu.SMEM((slots, peers), jnp.int32), pltpu.VMEM((rows, feats), F32),
         pltpu.SemaphoreType.DMA((10,))),
        mib=FULL,
    )(send, node_feats, w_query, w_key, w_value, w_out, cotangent, edge_dst, edge_src, edge_mask)
    arrived = lax.all_to_all(picked, "nodes", split_axis=0, concat_axis=0, tiled=True)
    heads = like((EARLY, rows, rows), BF16)
    low, far_count, near_count, w, g = call(
        local_kernel,
        (like((6, rows, feats), BF16), like((rows, width), F32), like((rows, rows), F32),
         heads, heads),
        [VMEM] * 3,
        cost=cost,
    )(gain, squares, edges)
    att, near, keep, give = call(
        attend_kernel,
        (square, wide, like((chips, block, feats), F32), like((chips, block, feats), BF16)),
        [VMEM] * 8,
        [
            pltpu.VMEM((HEADS, rows, rows + width), BF16),
            pltpu.VMEM((HEADS, rows, rows + width), BF16),
            pltpu.VMEM((feats, rows + width), F32),
            pltpu.VMEM((feats, rows + width), F32),
            pltpu.VMEM((4 * feats, feats), F32),
        ],
    )(arrived, gain, squares, low, far_count, near_count, w, g)
    given = lax.ppermute(give, "nodes", swap)
    output, own = call(own_kernel, (square, wide), [VMEM] * 4, cost=cost)(
        squares, gain, near, att
    )
    given, own = lax.optimization_barrier((given, own))
    paired = call(
        functools.partial(pair_kernel, share, slots),
        like((chips, message, feats), BF16),
        [VMEM] * 2,
    )(keep, given)
    got = across(paired)
    shares = call(reduce_kernel, like((chips, share, feats), BF16), [VMEM])(got)
    mine = across(shares)
    other = lax.ppermute(mine, "nodes", swap)
    grad_feats = call(
        functools.partial(finish_kernel, share), wide, [SMEM] + [VMEM] * 2, cost=cost
    )(send, got, own)
    *grads, grad_gain = call(
        spread_kernel, (like((feats, feats), F32),) * 4 + (like((1, feats), F32),), [VMEM] * 6
    )(mine, other, gain, w_query, w_key, w_value)
    return (output, grad_feats, grad_gain.reshape(feats), *grads)


def solution(mesh):
    nodes = P(("groups", "nodes"), None)
    in_specs = (
        nodes, P(), P(), P(), P(), P(), nodes, nodes, nodes, nodes,
        P(("groups", "nodes"), None, None),
    )
    out_specs = (nodes, nodes, P("groups")) + (P("groups", None),) * 4
    return jax.shard_map(
        on_device, mesh=mesh, in_specs=in_specs, out_specs=out_specs, check_vma=False
    )
```

```python
import functools
import math

import jax
import jax.numpy as jnp
from jax import lax
from jax.experimental import pallas as pl
from jax.experimental.pallas import tpu as pltpu
from jax.sharding import PartitionSpec as P

HEADS = 8
EARLY = 4
EPS = 1e-05
F32 = jnp.float32
BF16 = jnp.bfloat16
VMEM = pl.BlockSpec(memory_space=pltpu.VMEM)
SMEM = pl.BlockSpec(memory_space=pltpu.SMEM)
HBM = pl.BlockSpec(memory_space=pltpu.HBM)
MIB = 1024 * 1024
FULL = 60


def up(n, m):
    return -(-n // m) * m


def dot(a, b):
    return jnp.dot(a, b, preferred_element_type=F32)


def dot_t(a, b):
    return lax.dot_general(a, b, (((1,), (1,)), ((), ())), preferred_element_type=F32)


def standardize(x):
    centered = x - jnp.mean(x, axis=1, keepdims=True)
    rstd = lax.rsqrt(jnp.mean(centered * centered, axis=1, keepdims=True) + EPS)
    return centered * rstd, rstd


def pull(g, xhat, rstd):
    mean_g = jnp.mean(g, axis=1, keepdims=True)
    mean_gx = jnp.mean(g * xhat, axis=1, keepdims=True)
    return rstd * (g - mean_g - xhat * mean_gx)


def begin(sources, targets, sems):
    copies = [
        pltpu.make_async_copy(source, target, sems.at[i])
        for i, (source, target) in enumerate(zip(sources, targets))
    ]
    for copy in copies:
        copy.start()
    return copies


def finish_all(copies):
    for copy in copies:
        copy.wait()


def pick_kernel(send_hbm, *refs):
    squares = refs[:6]
    small = refs[6:10]
    out_ref, pack_ref, send, wide, dst_ref, src_ref, mask_ref, gain_ref, sems = refs[10:]
    copies = begin(
        (send_hbm,) + squares + small,
        [send] + [pack_ref.at[i] for i in range(6)] + [dst_ref, src_ref, mask_ref, gain_ref],
        sems,
    )
    finish_all(copies[:2])
    slots, peers = send.shape
    rows, feats = wide.shape
    wide[...] = pack_ref[0].astype(F32)
    for peer in range(peers):
        picked = [wide[pl.ds(send[slot, peer], 1), :] for slot in range(slots)]
        out_ref[peer] = jnp.concatenate(picked, axis=0).astype(BF16)
    finish_all(copies[7:])
    src = jnp.where(mask_ref[...] > 0, src_ref[...], -1)
    parts = [dst_ref[...].astype(F32)]
    for base in range(0, rows + up(slots * peers, 128), rows):
        inside = (src >= base) & (src < base + rows)
        parts.append(jnp.where(inside, src - base, -1).astype(F32))
    if len(parts) % 2:
        parts.append(parts[0])
    tall = [jnp.concatenate(parts[i : i + 2], axis=1) for i in range(0, len(parts), 2)]
    gain = gain_ref[...]
    first = gain.astype(BF16).astype(F32)
    second = (gain - first).astype(BF16).astype(F32)
    gains = [first, second, gain - first - second]
    used = sum(t.shape[0] for t in tall)
    blank = jnp.zeros((rows - used - 3, feats), F32)
    pack_ref[6] = jnp.concatenate(tall + gains + [blank], axis=0).astype(BF16)
    finish_all(copies[2:7])


def gain_row(edge_rows, rows, width):
    tables = 1 + -(-(rows + width) // rows)
    return up(tables, 2) // 2 * edge_rows


def packed_gain(pack_ref, at):
    parts = pack_ref[6].astype(F32)[at : at + 3]
    return parts[0:1] + parts[1:2] + parts[2:3]


def head_hots(feats):
    lane = lax.broadcasted_iota(jnp.int32, (1, feats), 1)
    size = feats // HEADS
    masks = [(lane >= h * size) & (lane < (h + 1) * size) for h in range(HEADS)]
    return masks, [m.astype(F32).astype(BF16) for m in masks]


def weigh(queries, keys, count, head):
    t = jnp.tanh(dot_t(queries, keys) * (0.2 / math.sqrt(head)))
    w = count * jnp.exp(5.0 * t)
    return w.astype(BF16), (w * (1.0 - t * t) * (1.0 / math.sqrt(head))).astype(BF16)


def local_kernel(edge_rows, pack_ref, low_ref, far_count, near_count, w_ref, g_ref):
    x_ref, wq_ref, wk_ref, wv_ref, wo_ref, cot_ref = [pack_ref.at[i] for i in range(6)]
    rows, width = far_count.shape
    gain = packed_gain(pack_ref, gain_row(edge_rows, rows, width))
    queries, keys = local_project(
        x_ref, gain, wq_ref, wk_ref, wv_ref, wo_ref, cot_ref, low_ref
    )
    feats = queries.shape[1]
    local_count(edge_rows, pack_ref, far_count, near_count)
    _, hots = head_hots(feats)
    for h in range(EARLY):
        w_ref[h], g_ref[h] = weigh(queries * hots[h], keys, near_count[...], feats // HEADS)


def local_project(x_ref, gain, wq_ref, wk_ref, wv_ref, wo_ref, cot_ref, low_ref):
    xhat, _ = standardize(x_ref[...].astype(F32))
    normed = (xhat * gain).astype(BF16)
    queries = dot(normed, wq_ref[...]).astype(BF16)
    keys = dot(normed, wk_ref[...]).astype(BF16)
    low_ref[0] = queries
    low_ref[1] = keys
    low_ref[2] = dot(normed, wv_ref[...]).astype(BF16)
    low_ref[3] = queries.T
    low_ref[4] = normed.T
    low_ref[5] = dot_t(cot_ref[...], wo_ref[...]).astype(BF16)
    return queries, keys


def local_count(edge_rows, pack_ref, far_count, near_count):
    rows, far = far_count.shape
    edge = 128
    group = 8
    table = pack_ref[6].astype(F32)

    def part(i):
        at = i // 2 * edge_rows
        return table[at : at + edge_rows, i % 2 * edge : (i % 2 + 1) * edge]

    ids = lax.broadcasted_iota(jnp.int32, (rows, edge), 0).astype(F32)

    def hot(values, height, base):
        at = ids[:height]
        return jnp.concatenate(
            [(at == values[j : j + 1]).astype(F32).astype(BF16) for j in range(base, base + group)],
            axis=1,
        )

    row_id = lax.broadcasted_iota(jnp.int32, (rows, rows), 0)
    col_id = lax.broadcasted_iota(jnp.int32, (rows, rows), 1)
    spans = [(b, min(rows, rows + far - b)) for b in range(0, rows + far, rows)]
    totals = [jnp.zeros((rows, height), F32) for _, height in spans]
    totals[0] = (row_id == col_id).astype(F32)
    values = [part(i) for i in range(len(spans) + 1)]
    for base in range(0, edge_rows, group):
        hot_dst = hot(values[0], rows, base)
        for i, (_, height) in enumerate(spans):
            totals[i] = totals[i] + dot_t(hot_dst, hot(values[i + 1], height, base))
    near_count[...] = totals[0]
    for (b, height), total in zip(spans[1:], totals[1:]):
        far_count[:, b - rows : b - rows + height] = total


def attend_kernel(
    edge_rows, far_ref, pack_ref, low_ref, far_count, near_count, near_w, near_g,
    att_ref, near_ref, keep_ref, give_ref,
    w_scr, g_scr, dkt_scr, dvt_scr, grad_scr,
):
    _, wq_ref, wk_ref, wv_ref, _, cot_ref = [pack_ref.at[i] for i in range(6)]
    _, rows, feats = low_ref.shape
    q_ref, k_ref, v_ref, qt_ref, normt_ref, datt_ref = [low_ref.at[i] for i in range(6)]
    peers, slots, _ = far_ref.shape
    far = peers * slots
    width = far_count.shape[1]
    head = feats // HEADS
    chips, block, _ = keep_ref.shape
    pad = width - far
    far_x = jnp.concatenate([far_ref[p].astype(F32) for p in range(peers)], axis=0)
    if pad:
        far_x = jnp.concatenate([far_x, jnp.zeros((pad, feats), F32)], axis=0)
    gain = packed_gain(pack_ref, gain_row(edge_rows, rows, width))
    far_hat, far_rstd = standardize(far_x)
    far_normed = (far_hat * gain).astype(BF16)
    far_keys = dot(far_normed, wk_ref[...]).astype(BF16)
    far_values = dot(far_normed, wv_ref[...]).astype(BF16)
    keys = jnp.concatenate([k_ref[...], far_keys], axis=0)
    values = jnp.concatenate([v_ref[...], far_values], axis=0)
    masks, hots = head_hots(feats)
    queries = q_ref[...]
    count = far_count[...]
    both_count = jnp.concatenate([near_count[...], count], axis=1)
    num = jnp.zeros((rows, feats), F32)
    den = jnp.zeros((rows, feats), F32)
    for h in range(HEADS):
        q_head = queries * hots[h]
        if h < EARLY:
            w, g = weigh(q_head, far_keys, count, head)
            w = jnp.concatenate([near_w[h], w], axis=1)
            g = jnp.concatenate([near_g[h], g], axis=1)
        else:
            w, g = weigh(q_head, keys, both_count, head)
        w_scr[h] = w
        g_scr[h] = g
        num = num + dot(w, values * hots[h])
        den = den + dot(w, jnp.broadcast_to(hots[h], (rows + width, feats)))
    rden = 1.0 / den
    att32 = num * rden
    att = att32.astype(BF16)
    att_ref[...] = att
    grad_out = dot(att.T, cot_ref[...])
    dnum = (datt_ref[...].astype(F32) * rden).astype(BF16)
    dnum_t = dnum.T
    prod = dnum.astype(F32) * att32
    qt = qt_ref[...]
    dq = jnp.zeros((rows, feats), F32)
    for h in range(HEADS):
        z = jnp.sum(jnp.where(masks[h], prod, 0.0), axis=1, keepdims=True)
        dw = dot_t(dnum * hots[h], values) - z
        ds = (g_scr[h].astype(F32) * dw).astype(BF16)
        dq = dq + dot(ds, keys * hots[h])
        at = slice(h * head, (h + 1) * head)
        dkt_scr[at, :] = dot(qt[at, :], ds)
        dvt_scr[at, :] = dot(dnum_t[at, :], w_scr[h])
    dq = dq.astype(BF16)
    dkt = dkt_scr[...].astype(BF16)
    dvt = dvt_scr[...].astype(BF16)
    norm_t = jnp.concatenate([normt_ref[...], far_normed.T], axis=1)
    grad_query = dot(normt_ref[...], dq)
    grad_key = dot_t(norm_t, dkt)
    grad_value = dot_t(norm_t, dvt)
    d_normed = (dot(wk_ref[...], dkt) + dot(wv_ref[...], dvt)).T
    near = d_normed[:rows] + dot_t(dq, wq_ref[...])
    near_ref[...] = near
    away = d_normed[rows:]
    away_dx = pull(away * gain, far_hat, far_rstd)
    grad_scr[...] = jnp.concatenate([grad_query, grad_key, grad_value, grad_out], axis=0)
    half = grad_scr.shape[0] // 2
    share = half // chips
    blank = jnp.zeros((block - share - slots, feats), F32)
    core = lax.rem(lax.axis_index("nodes"), 2)
    for c in range(chips):
        for own in (True, False):
            which = core if own else 1 - core
            start = pl.multiple_of(which * half + c * share, 8)
            dx = [away_dx[(2 * c + i) * slots : (2 * c + i + 1) * slots] for i in range(2)]
            part = jnp.concatenate(
                [grad_scr[pl.ds(start, share), :], jnp.where(which == 0, dx[0], dx[1]), blank],
                axis=0,
            )
            if own:
                keep_ref[c] = part
            else:
                give_ref[c] = part.astype(BF16)


def pair_kernel(share, slots, keep_ref, got_ref, out_ref):
    chips, block, feats = out_ref.shape
    blank = [jnp.zeros((block - share - 2 * slots, feats), F32)] * (block > share + 2 * slots)
    for c in range(chips):
        keep = keep_ref[c]
        got = got_ref[c].astype(F32)
        end = share + slots
        out_ref[c] = jnp.concatenate(
            [keep[:share] + got[:share], keep[share:end], got[share:end]] + blank, axis=0
        ).astype(BF16)


def reduce_kernel(got_ref, share_ref):
    chips, share, _ = share_ref.shape
    total = jnp.zeros(share_ref.shape[1:], F32)
    for c in range(chips):
        total = total + got_ref[c].astype(F32)[:share]
    share_ref[...] = jnp.broadcast_to(total.astype(BF16)[None], share_ref.shape)


def own_kernel(gain_at, square_ref, near_ref, att_ref, out_ref, feats_ref):
    x = square_ref[0].astype(F32)
    out_ref[...] = (x + dot(att_ref[...], square_ref[4])).astype(BF16)
    gain = packed_gain(square_ref, gain_at)
    dx = pull(near_ref[...] * gain, *standardize(x))
    feats_ref[...] = square_ref[5].astype(F32) + dx


def finish_kernel(share, send_ref, got_ref, own_ref, feats_ref):
    slots, peers = send_ref.shape
    feats_ref[...] = own_ref[...]
    core = lax.rem(lax.axis_index("nodes"), 2)
    for c in range(peers // 2):
        got = got_ref[c].astype(F32)
        for i in range(2 * slots):
            peer = 2 * c + (core if i < slots else 1 - core)
            at = pl.ds(send_ref[i % slots, peer], 1)
            feats_ref[at, :] += got[share + i : share + i + 1]


def spread_kernel(mine_ref, other_ref, gain_ref, wq_ref, wk_ref, wv_ref, *out_refs):
    rows = wq_ref.shape[0]
    chips, share, feats = mine_ref.shape
    first = lax.rem(lax.axis_index("nodes"), 2) == 0
    mine = mine_ref[...].astype(F32).reshape(chips * share, feats)
    other = other_ref[...].astype(F32).reshape(chips * share, feats)
    low = jnp.where(first, mine, other)
    high = jnp.where(first, other, mine)
    grads = (low[:rows], low[rows:], high[:rows], high[rows:])
    for grad, out_ref in zip(grads, out_refs):
        out_ref[...] = grad
    prod = jnp.zeros((rows, feats), F32)
    for grad, w_ref in zip(grads, (wq_ref, wk_ref, wv_ref)):
        prod = prod + grad * w_ref[...].astype(F32)
    out_refs[4][...] = jnp.sum(prod.T, axis=0, keepdims=True) / gain_ref[...]


def call(kernel, out_shape, in_specs, scratch=(), cost=None, out_specs=None, mib=16):
    return pl.pallas_call(
        kernel,
        out_shape=out_shape,
        in_specs=in_specs,
        out_specs=jax.tree.map(lambda _: VMEM, out_shape) if out_specs is None else out_specs,
        scratch_shapes=list(scratch),
        compiler_params=pltpu.CompilerParams(vmem_limit_bytes=mib * MIB),
        cost_estimate=cost,
    )


def on_device(
    node_feats, norm_gain, w_query, w_key, w_value, w_out, cotangent,
    edge_dst, edge_src, edge_mask, send_rows,
):
    rows, feats = node_feats.shape
    peers, slots = send_rows.shape[1:]
    far = peers * slots
    width = up(far, 128)
    chips = peers // 2
    share = 2 * feats // chips
    block = up(share + slots, 8)
    message = up(share + 2 * slots, 8)
    gain = norm_gain.reshape(1, feats)
    send = send_rows[0].T
    swap = [(i, i ^ 1) for i in range(peers)]
    sides = [list(range(k, peers, 2)) for k in range(2)]

    def like(shape, dtype):
        return jax.ShapeDtypeStruct(shape, dtype)

    def across(x):
        return lax.all_to_all(x, "nodes", 0, 0, axis_index_groups=sides, tiled=True)

    cost = pl.CostEstimate(flops=8_000_000_000, bytes_accessed=2_000_000, transcendentals=0)
    square = like((rows, feats), BF16)
    wide = like((rows, feats), F32)
    edges = edge_dst.shape
    ints = pltpu.VMEM(edges, jnp.int32)
    picked, pack = call(
        pick_kernel,
        (like((peers, slots, feats), BF16), like((7, rows, feats), BF16)),
        [HBM] * 11,
        (pltpu.SMEM((slots, peers), jnp.int32), pltpu.VMEM((rows, feats), F32), ints, ints, ints,
         pltpu.VMEM((1, feats), F32), pltpu.SemaphoreType.DMA((11,))),
        mib=FULL,
    )(send, node_feats, w_query, w_key, w_value, w_out, cotangent, edge_dst, edge_src, edge_mask,
      gain)
    arrived = lax.all_to_all(picked, "nodes", split_axis=0, concat_axis=0, tiled=True)
    heads = like((EARLY, rows, rows), BF16)
    low, far_count, near_count, w, g = call(
        functools.partial(local_kernel, edges[0]),
        (like((6, rows, feats), BF16), like((rows, width), F32), like((rows, rows), F32),
         heads, heads),
        [VMEM],
        cost=cost,
    )(pack)
    att, near, keep, give = call(
        functools.partial(attend_kernel, edges[0]),
        (square, wide, like((chips, block, feats), F32), like((chips, block, feats), BF16)),
        [VMEM] * 7,
        [
            pltpu.VMEM((HEADS, rows, rows + width), BF16),
            pltpu.VMEM((HEADS, rows, rows + width), BF16),
            pltpu.VMEM((feats, rows + width), F32),
            pltpu.VMEM((feats, rows + width), F32),
            pltpu.VMEM((4 * feats, feats), F32),
        ],
    )(arrived, pack, low, far_count, near_count, w, g)
    given = lax.ppermute(give, "nodes", swap)
    output, own = call(
        functools.partial(own_kernel, gain_row(edges[0], rows, width)),
        (square, wide),
        [VMEM] * 3,
        cost=cost,
    )(pack, near, att)
    given, own = lax.optimization_barrier((given, own))
    paired = call(
        functools.partial(pair_kernel, share, slots),
        like((chips, message, feats), BF16),
        [VMEM] * 2,
    )(keep, given)
    got = across(paired)
    shares = call(reduce_kernel, like((chips, share, feats), BF16), [VMEM])(got)
    mine = across(shares)
    other = lax.ppermute(mine, "nodes", swap)
    grad_feats = call(
        functools.partial(finish_kernel, share), wide, [SMEM] + [VMEM] * 2, cost=cost
    )(send, got, own)
    *grads, grad_gain = call(
        spread_kernel, (like((feats, feats), F32),) * 4 + (like((1, feats), F32),), [VMEM] * 6
    )(mine, other, gain, w_query, w_key, w_value)
    return (output, grad_feats, grad_gain.reshape(feats), *grads)


def solution(mesh):
    nodes = P(("groups", "nodes"), None)
    in_specs = (
        nodes, P(), P(), P(), P(), P(), nodes, nodes, nodes, nodes,
        P(("groups", "nodes"), None, None),
    )
    out_specs = (nodes, nodes, P("groups")) + (P("groups", None),) * 4
    return jax.shard_map(
        on_device, mesh=mesh, in_specs=in_specs, out_specs=out_specs, check_vma=False
    )
```

```python
import functools
import math

import jax
import jax.numpy as jnp
from jax import lax
from jax.experimental import pallas as pl
from jax.experimental.pallas import tpu as pltpu
from jax.sharding import PartitionSpec as P

HEADS = 8
EARLY = 4
EPS = 1e-05
F32 = jnp.float32
BF16 = jnp.bfloat16
VMEM = pl.BlockSpec(memory_space=pltpu.VMEM)
SMEM = pl.BlockSpec(memory_space=pltpu.SMEM)
MIB = 1024 * 1024
FULL = 60


def up(n, m):
    return -(-n // m) * m


def dot(a, b):
    return jnp.dot(a, b, preferred_element_type=F32)


def dot_t(a, b):
    return lax.dot_general(a, b, (((1,), (1,)), ((), ())), preferred_element_type=F32)


def standardize(x):
    centered = x - jnp.mean(x, axis=1, keepdims=True)
    rstd = lax.rsqrt(jnp.mean(centered * centered, axis=1, keepdims=True) + EPS)
    return centered * rstd, rstd


def pull(g, xhat, rstd):
    mean_g = jnp.mean(g, axis=1, keepdims=True)
    mean_gx = jnp.mean(g * xhat, axis=1, keepdims=True)
    return rstd * (g - mean_g - xhat * mean_gx)


def pick_kernel(send_ref, *refs):
    squares = refs[:6]
    dst_ref, src_ref, mask_ref, gain_ref, out_ref, pack_ref, wide = refs[6:]
    slots, peers = send_ref.shape
    rows, feats = wide.shape
    wide[...] = squares[0][...].astype(F32)
    for i, square in enumerate(squares):
        pack_ref[i] = square[...]
    for peer in range(peers):
        picked = [wide[pl.ds(send_ref[slot, peer], 1), :] for slot in range(slots)]
        out_ref[peer] = jnp.concatenate(picked, axis=0).astype(BF16)
    src = jnp.where(mask_ref[...] > 0, src_ref[...], -1)
    parts = [dst_ref[...].astype(F32)]
    for base in range(0, rows + up(slots * peers, 128), rows):
        inside = (src >= base) & (src < base + rows)
        parts.append(jnp.where(inside, src - base, -1).astype(F32))
    if len(parts) % 2:
        parts.append(parts[0])
    tall = [jnp.concatenate(parts[i : i + 2], axis=1) for i in range(0, len(parts), 2)]
    gain = gain_ref[...]
    first = gain.astype(BF16).astype(F32)
    second = (gain - first).astype(BF16).astype(F32)
    gains = [first, second, gain - first - second]
    used = sum(t.shape[0] for t in tall)
    blank = jnp.zeros((rows - used - 3, feats), F32)
    pack_ref[6] = jnp.concatenate(tall + gains + [blank], axis=0).astype(BF16)


def gain_row(edge_rows, rows, width):
    tables = 1 + -(-(rows + width) // rows)
    return up(tables, 2) // 2 * edge_rows


def packed_gain(pack_ref, at):
    parts = pack_ref[6].astype(F32)[at : at + 3]
    return parts[0:1] + parts[1:2] + parts[2:3]


def head_hots(feats):
    lane = lax.broadcasted_iota(jnp.int32, (1, feats), 1)
    size = feats // HEADS
    masks = [(lane >= h * size) & (lane < (h + 1) * size) for h in range(HEADS)]
    return masks, [m.astype(F32).astype(BF16) for m in masks]


def weigh(queries, keys, count, head):
    t = jnp.tanh(dot_t(queries, keys) * (0.2 / math.sqrt(head)))
    w = count * jnp.exp2(t * (5.0 / math.log(2.0)))
    return w.astype(BF16), (w * (1.0 - t * t)).astype(BF16)


def local_kernel(edge_rows, pack_ref, low_ref, far_count, near_count, w_ref, g_ref):
    x_ref, wq_ref, wk_ref, wv_ref, wo_ref, cot_ref = [pack_ref.at[i] for i in range(6)]
    rows, width = far_count.shape
    gain = packed_gain(pack_ref, gain_row(edge_rows, rows, width))
    queries, keys = local_project(
        x_ref, gain, wq_ref, wk_ref, wv_ref, wo_ref, cot_ref, low_ref
    )
    feats = queries.shape[1]
    local_count(edge_rows, pack_ref, far_count, near_count)
    _, hots = head_hots(feats)
    for h in range(EARLY):
        w_ref[h], g_ref[h] = weigh(queries * hots[h], keys, near_count[...], feats // HEADS)


def local_project(x_ref, gain, wq_ref, wk_ref, wv_ref, wo_ref, cot_ref, low_ref):
    xhat, _ = standardize(x_ref[...].astype(F32))
    normed = (xhat * gain).astype(BF16)
    queries = dot(normed, wq_ref[...]).astype(BF16)
    keys = dot(normed, wk_ref[...]).astype(BF16)
    low_ref[0] = queries
    low_ref[1] = keys
    low_ref[2] = dot(normed, wv_ref[...]).astype(BF16)
    low_ref[3] = queries.T
    low_ref[4] = normed.T
    low_ref[5] = dot_t(cot_ref[...], wo_ref[...]).astype(BF16)
    return queries, keys


def local_count(edge_rows, pack_ref, far_count, near_count):
    rows, far = far_count.shape
    edge = 128
    group = 8
    table = pack_ref[6].astype(F32)

    def part(i):
        at = i // 2 * edge_rows
        return table[at : at + edge_rows, i % 2 * edge : (i % 2 + 1) * edge]

    ids = lax.broadcasted_iota(jnp.int32, (rows, edge), 0).astype(F32)

    def hot(values, height, base):
        at = ids[:height]
        return jnp.concatenate(
            [(at == values[j : j + 1]).astype(F32).astype(BF16) for j in range(base, base + group)],
            axis=1,
        )

    row_id = lax.broadcasted_iota(jnp.int32, (rows, rows), 0)
    col_id = lax.broadcasted_iota(jnp.int32, (rows, rows), 1)
    spans = [(b, min(rows, rows + far - b)) for b in range(0, rows + far, rows)]
    totals = [jnp.zeros((rows, height), F32) for _, height in spans]
    totals[0] = (row_id == col_id).astype(F32)
    values = [part(i) for i in range(len(spans) + 1)]
    for base in range(0, edge_rows, group):
        hot_dst = hot(values[0], rows, base)
        for i, (_, height) in enumerate(spans):
            totals[i] = totals[i] + dot_t(hot_dst, hot(values[i + 1], height, base))
    near_count[...] = totals[0]
    for (b, height), total in zip(spans[1:], totals[1:]):
        far_count[:, b - rows : b - rows + height] = total


def attend_kernel(
    edge_rows, far_ref, pack_ref, low_ref, far_count, near_count, near_w, near_g,
    tail_ref, keep_ref, give_ref,
    w_scr, g_scr, far_w, far_g, dkt_scr, dvt_scr,
):
    _, wq_ref, wk_ref, wv_ref, _, cot_ref = [pack_ref.at[i] for i in range(6)]
    _, rows, feats = low_ref.shape
    queries, keys, values, qt, norm_t, datt = [low_ref[i] for i in range(6)]
    peers, slots, _ = far_ref.shape
    far = peers * slots
    width = far_count.shape[1]
    head = feats // HEADS
    pairs = HEADS // 2
    chips, block, _ = keep_ref.shape
    pad = width - far
    far_x = jnp.concatenate([far_ref[p].astype(F32) for p in range(peers)], axis=0)
    if pad:
        far_x = jnp.concatenate([far_x, jnp.zeros((pad, feats), F32)], axis=0)
    gain = packed_gain(pack_ref, gain_row(edge_rows, rows, width))
    far_hat, far_rstd = standardize(far_x)
    far_normed = (far_hat * gain).astype(BF16)
    far_keys = dot(far_normed, wk_ref[...]).astype(BF16)
    far_values = dot(far_normed, wv_ref[...]).astype(BF16)
    masks, hots = head_hots(feats)
    lane = lax.broadcasted_iota(jnp.int32, (1, feats), 1)
    even = lax.rem(lane // (2 * head), 2) == 0

    def both(x, j):
        return jnp.concatenate([x * hots[2 * j], x * hots[2 * j + 1]], axis=0)

    def summed(h):
        return hots[h + 2] if h // 2 % 2 == 0 else hots[h - 2]

    count = jnp.concatenate([far_count[...]] * 2, axis=1)
    near = near_count[...]
    seen = [[], []]
    for j in range(pairs):
        w, far_g[j] = weigh(queries, both(far_keys, j), count, head)
        far_w[j] = w
        side = j % 2
        far_ones = jnp.concatenate(
            [jnp.broadcast_to(summed(h), (width, feats)) for h in (2 * j, 2 * j + 1)], axis=0
        )
        seen[side].append((w, both(far_values, j) + far_ones))
        for h in (2 * j, 2 * j + 1):
            if h < EARLY:
                w = near_w[h]
            else:
                w, g_scr[h - EARLY] = weigh(queries * hots[h], keys, near, head)
                w_scr[h - EARLY] = w
            seen[side].append((w, values * hots[h] + summed(h)))
    total = [
        dot(
            jnp.concatenate([w for w, _ in side], axis=1),
            jnp.concatenate([v for _, v in side], axis=0),
        )
        for side in seen
    ]
    num = jnp.where(even, total[0], total[1])
    crossed = jnp.where(even, total[1], total[0])
    den = jnp.concatenate(
        [pltpu.roll(crossed[:, i : i + 4 * head], 2 * head, 1) for i in range(0, feats, 4 * head)],
        axis=1,
    )
    rden = 1.0 / den
    att32 = num * rden
    att = att32.astype(BF16)
    tail_ref[0] = att
    grad_out = dot(att.T, cot_ref[...])
    dnum = (datt.astype(F32) * rden).astype(BF16)
    dnum_t = dnum.T
    prod = dnum.astype(F32) * att32
    dq = jnp.zeros((rows, feats), F32)
    slopes, weights, far_slopes = [], [], []
    for j in range(pairs):
        z = [
            jnp.sum(jnp.where(masks[h], prod, 0.0), axis=1, keepdims=True)
            for h in (2 * j, 2 * j + 1)
        ]
        far_z = jnp.concatenate([jnp.broadcast_to(x, (rows, width)) for x in z], axis=1)
        dw = dot_t(dnum, both(far_values, j)) - far_z
        ds = (far_g[j].astype(F32) * dw).astype(BF16)
        dq = dq + dot(ds, both(far_keys, j))
        far_slopes.append(ds)
        for i, h in enumerate((2 * j, 2 * j + 1)):
            w, g = (near_w[h], near_g[h]) if h < EARLY else (w_scr[h - EARLY], g_scr[h - EARLY])
            dw = dot_t(dnum * hots[h], values) - z[i]
            ds = (g.astype(F32) * dw).astype(BF16)
            dq = dq + dot(ds, keys * hots[h])
            slopes.append(ds)
            weights.append(w)
    for h in range(HEADS):
        at = slice(h * head, (h + 1) * head)
        dkt_scr[at, :rows] = dot(qt[at, :], slopes[h])
        dvt_scr[at, :rows] = dot(dnum_t[at, :], weights[h])
    for j in range(pairs):
        at = slice(2 * j * head, (2 * j + 2) * head)
        dk = dot(qt[at, :], far_slopes[j])
        dv = dot(dnum_t[at, :], far_w[j])
        for i in range(2):
            at = slice((2 * j + i) * head, (2 * j + i + 1) * head)
            part = slice(i * head, (i + 1) * head)
            cols = slice(i * width, (i + 1) * width)
            dkt_scr[at, rows:] = dk[part, cols]
            dvt_scr[at, rows:] = dv[part, cols]
    slope = 1.0 / math.sqrt(head)
    dq = (dq * slope).astype(BF16)
    dkt = (dkt_scr[...] * slope).astype(BF16)
    dvt = dvt_scr[...].astype(BF16)
    tail_ref[1] = dq
    tail_ref[2] = dkt[:, :rows]
    tail_ref[3] = dvt[:, :rows]
    all_t = jnp.concatenate([norm_t, far_normed.T], axis=1)
    grad_query = dot(norm_t, dq)
    grad_key = dot_t(all_t, dkt)
    grad_value = dot_t(all_t, dvt)
    away = (dot(wk_ref[...], dkt[:, rows:]) + dot(wv_ref[...], dvt[:, rows:])).T
    away_dx = pull(away * gain, far_hat, far_rstd)
    share = 2 * feats // chips
    blank = [jnp.zeros((block - share - slots, feats), F32)] * (block > share + slots)
    first = lax.rem(lax.axis_index("nodes"), 2) == 0
    low = jnp.concatenate([grad_query, grad_key], axis=0)
    high = jnp.concatenate([grad_value, grad_out], axis=0)
    keep = jnp.where(first, low, high)
    give = jnp.where(first, high, low)
    for c in range(chips):
        dx = [away_dx[(2 * c + i) * slots : (2 * c + i + 1) * slots] for i in range(2)]
        at = slice(c * share, (c + 1) * share)
        keep_ref[c] = jnp.concatenate(
            [keep[at], jnp.where(first, dx[0], dx[1])] + blank, axis=0
        )
        give_ref[c] = jnp.concatenate(
            [give[at], jnp.where(first, dx[1], dx[0])] + blank, axis=0
        ).astype(BF16)


def pair_kernel(share, slots, keep_ref, got_ref, out_ref):
    chips, block, feats = out_ref.shape
    blank = [jnp.zeros((block - share - 2 * slots, feats), F32)] * (block > share + 2 * slots)
    for c in range(chips):
        keep = keep_ref[c]
        got = got_ref[c].astype(F32)
        end = share + slots
        out_ref[c] = jnp.concatenate(
            [keep[:share] + got[:share], keep[share:end], got[share:end]] + blank, axis=0
        ).astype(BF16)


def reduce_kernel(got_ref, share_ref):
    chips, share, _ = share_ref.shape
    total = jnp.zeros(share_ref.shape[1:], F32)
    for c in range(chips):
        total = total + got_ref[c].astype(F32)[:share]
    share_ref[...] = jnp.broadcast_to(total.astype(BF16)[None], share_ref.shape)


def own_kernel(gain_at, pack_ref, tail_ref, out_ref, feats_ref):
    x_ref, wq_ref, wk_ref, wv_ref, wo_ref, cot_ref = [pack_ref.at[i] for i in range(6)]
    x = x_ref[...].astype(F32)
    out_ref[...] = (x + dot(tail_ref[0], wo_ref[...])).astype(BF16)
    d_normed = (dot(wk_ref[...], tail_ref[2]) + dot(wv_ref[...], tail_ref[3])).T
    d_normed = d_normed + dot_t(tail_ref[1], wq_ref[...])
    gain = packed_gain(pack_ref, gain_at)
    feats_ref[...] = cot_ref[...].astype(F32) + pull(d_normed * gain, *standardize(x))


def finish_kernel(share, send_ref, got_ref, own_ref, feats_ref):
    slots, peers = send_ref.shape
    feats_ref[...] = own_ref[...]
    core = lax.rem(lax.axis_index("nodes"), 2)
    for c in range(peers // 2):
        got = got_ref[c].astype(F32)
        for i in range(2 * slots):
            peer = 2 * c + (core if i < slots else 1 - core)
            at = pl.ds(send_ref[i % slots, peer], 1)
            feats_ref[at, :] += got[share + i : share + i + 1]


def spread_kernel(mine_ref, other_ref, gain_ref, wq_ref, wk_ref, wv_ref, *out_refs):
    rows = wq_ref.shape[0]
    chips, share, feats = mine_ref.shape
    first = lax.rem(lax.axis_index("nodes"), 2) == 0
    mine = mine_ref[...].astype(F32).reshape(chips * share, feats)
    other = other_ref[...].astype(F32).reshape(chips * share, feats)
    low = jnp.where(first, mine, other)
    high = jnp.where(first, other, mine)
    grads = (low[:rows], low[rows:], high[:rows], high[rows:])
    for grad, out_ref in zip(grads, out_refs):
        out_ref[...] = grad
    prod = jnp.zeros((rows, feats), F32)
    for grad, w_ref in zip(grads, (wq_ref, wk_ref, wv_ref)):
        prod = prod + grad * w_ref[...].astype(F32)
    out_refs[4][...] = jnp.sum(prod.T, axis=0, keepdims=True) / gain_ref[...]


def call(kernel, out_shape, in_specs, scratch=(), cost=None, out_specs=None, mib=16):
    return pl.pallas_call(
        kernel,
        out_shape=out_shape,
        in_specs=in_specs,
        out_specs=jax.tree.map(lambda _: VMEM, out_shape) if out_specs is None else out_specs,
        scratch_shapes=list(scratch),
        compiler_params=pltpu.CompilerParams(vmem_limit_bytes=mib * MIB),
        cost_estimate=cost,
    )


def on_device(
    node_feats, norm_gain, w_query, w_key, w_value, w_out, cotangent,
    edge_dst, edge_src, edge_mask, send_rows,
):
    rows, feats = node_feats.shape
    peers, slots = send_rows.shape[1:]
    far = peers * slots
    width = up(far, 128)
    chips = peers // 2
    share = 2 * feats // chips
    block = up(share + slots, 8)
    message = up(share + 2 * slots, 8)
    gain = norm_gain.reshape(1, feats)
    send = send_rows[0].T
    swap = [(i, i ^ 1) for i in range(peers)]
    sides = [list(range(k, peers, 2)) for k in range(2)]

    def like(shape, dtype):
        return jax.ShapeDtypeStruct(shape, dtype)

    def across(x):
        return lax.all_to_all(x, "nodes", 0, 0, axis_index_groups=sides, tiled=True)

    cost = pl.CostEstimate(flops=8_000_000_000, bytes_accessed=2_000_000, transcendentals=0)
    square = like((rows, feats), BF16)
    wide = like((rows, feats), F32)
    edges = edge_dst.shape
    picked, pack = call(
        pick_kernel,
        (like((peers, slots, feats), BF16), like((7, rows, feats), BF16)),
        [SMEM] + [VMEM] * 10,
        (pltpu.VMEM((rows, feats), F32),),
        mib=FULL,
    )(send, node_feats, w_query, w_key, w_value, w_out, cotangent, edge_dst, edge_src, edge_mask,
      gain)
    arrived = lax.all_to_all(picked, "nodes", split_axis=0, concat_axis=0, tiled=True)
    heads = like((EARLY, rows, rows), BF16)
    low, far_count, near_count, w, g = call(
        functools.partial(local_kernel, edges[0]),
        (like((6, rows, feats), BF16), like((rows, width), F32), like((rows, rows), F32),
         heads, heads),
        [VMEM],
        cost=cost,
    )(pack)
    late = pltpu.VMEM((max(HEADS - EARLY, 1), rows, rows), BF16)
    far_heads = pltpu.VMEM((HEADS // 2, rows, 2 * width), BF16)
    turned = pltpu.VMEM((feats, rows + width), F32)
    tail, keep, give = call(
        functools.partial(attend_kernel, edges[0]),
        (like((4, rows, feats), BF16), like((chips, block, feats), F32),
         like((chips, block, feats), BF16)),
        [VMEM] * 7,
        [late, late, far_heads, far_heads, turned, turned],
    )(arrived, pack, low, far_count, near_count, w, g)
    given = lax.ppermute(give, "nodes", swap)
    output, own = call(
        functools.partial(own_kernel, gain_row(edges[0], rows, width)),
        (square, wide),
        [VMEM] * 2,
        cost=cost,
    )(pack, tail)
    given, own = lax.optimization_barrier((given, own))
    paired = call(
        functools.partial(pair_kernel, share, slots),
        like((chips, message, feats), BF16),
        [VMEM] * 2,
    )(keep, given)
    got = across(paired)
    shares = call(reduce_kernel, like((chips, share, feats), BF16), [VMEM])(got)
    mine = across(shares)
    other = lax.ppermute(mine, "nodes", swap)
    grad_feats = call(
        functools.partial(finish_kernel, share), wide, [SMEM] + [VMEM] * 2, cost=cost
    )(send, got, own)
    *grads, grad_gain = call(
        spread_kernel, (like((feats, feats), F32),) * 4 + (like((1, feats), F32),), [VMEM] * 6
    )(mine, other, gain, w_query, w_key, w_value)
    return (output, grad_feats, grad_gain.reshape(feats), *grads)


def solution(mesh):
    nodes = P(("groups", "nodes"), None)
    in_specs = (
        nodes, P(), P(), P(), P(), P(), nodes, nodes, nodes, nodes,
        P(("groups", "nodes"), None, None),
    )
    out_specs = (nodes, nodes, P("groups")) + (P("groups", None),) * 4
    return jax.shard_map(
        on_device, mesh=mesh, in_specs=in_specs, out_specs=out_specs, check_vma=False
    )
```

```python
import functools
import math

import jax
import jax.numpy as jnp
from jax import lax
from jax.experimental import pallas as pl
from jax.experimental.pallas import tpu as pltpu
from jax.sharding import PartitionSpec as P

HEADS = 8
EARLY = 5
EPS = 1e-05
F32 = jnp.float32
BF16 = jnp.bfloat16
VMEM = pl.BlockSpec(memory_space=pltpu.VMEM)
SMEM = pl.BlockSpec(memory_space=pltpu.SMEM)
MIB = 1024 * 1024
FULL = 60


def up(n, m):
    return -(-n // m) * m


def dot(a, b):
    return jnp.dot(a, b, preferred_element_type=F32)


def dot_t(a, b):
    return lax.dot_general(a, b, (((1,), (1,)), ((), ())), preferred_element_type=F32)


def standardize(x):
    centered = x - jnp.mean(x, axis=1, keepdims=True)
    rstd = lax.rsqrt(jnp.mean(centered * centered, axis=1, keepdims=True) + EPS)
    return centered * rstd, rstd


def pull(g, xhat, rstd):
    mean_g = jnp.mean(g, axis=1, keepdims=True)
    mean_gx = jnp.mean(g * xhat, axis=1, keepdims=True)
    return rstd * (g - mean_g - xhat * mean_gx)


def pick_kernel(send_ref, *refs):
    squares = refs[:4]
    dst_ref, src_ref, mask_ref, gain_ref, out_ref, pack_ref, wide = refs[4:]
    slots, peers = send_ref.shape
    rows, feats = wide.shape
    wide[...] = squares[0][...].astype(F32)
    for i, square in enumerate(squares):
        pack_ref[i] = square[...]
    for peer in range(peers):
        picked = [wide[pl.ds(send_ref[slot, peer], 1), :] for slot in range(slots)]
        out_ref[peer] = jnp.concatenate(picked, axis=0).astype(BF16)
    src = jnp.where(mask_ref[...] > 0, src_ref[...], -1)
    parts = [dst_ref[...].astype(F32)]
    for base in range(0, rows + up(slots * peers, 128), rows):
        inside = (src >= base) & (src < base + rows)
        parts.append(jnp.where(inside, src - base, -1).astype(F32))
    if len(parts) % 2:
        parts.append(parts[0])
    tall = [jnp.concatenate(parts[i : i + 2], axis=1) for i in range(0, len(parts), 2)]
    gain = gain_ref[...]
    first = gain.astype(BF16).astype(F32)
    second = (gain - first).astype(BF16).astype(F32)
    gains = [first, second, gain - first - second]
    used = sum(t.shape[0] for t in tall)
    blank = jnp.zeros((rows - used - 3, feats), F32)
    pack_ref[4] = jnp.concatenate(tall + gains + [blank], axis=0).astype(BF16)


def gain_row(edge_rows, rows, width):
    tables = 1 + -(-(rows + width) // rows)
    return up(tables, 2) // 2 * edge_rows


def packed_gain(pack_ref, at):
    parts = pack_ref[4].astype(F32)[at : at + 3]
    return parts[0:1] + parts[1:2] + parts[2:3]


def head_hots(feats):
    lane = lax.broadcasted_iota(jnp.int32, (1, feats), 1)
    size = feats // HEADS
    masks = [(lane >= h * size) & (lane < (h + 1) * size) for h in range(HEADS)]
    return masks, [m.astype(F32).astype(BF16) for m in masks]


def weigh(queries, keys, count, head):
    t = jnp.tanh(dot_t(queries, keys) * (0.2 / math.sqrt(head)))
    w = count * jnp.exp2(t * (5.0 / math.log(2.0)))
    return w.astype(BF16), (w * (1.0 - t * t)).astype(BF16)


def local_kernel(edge_rows, pack_ref, low_ref, far_count, near_count, w_ref, g_ref):
    x_ref, wq_ref, wk_ref, wv_ref = [pack_ref.at[i] for i in range(4)]
    rows, width = far_count.shape
    gain = packed_gain(pack_ref, gain_row(edge_rows, rows, width))
    queries, keys = local_project(
        x_ref, gain, wq_ref, wk_ref, wv_ref, low_ref
    )
    feats = queries.shape[1]
    local_count(edge_rows, pack_ref, far_count, near_count)
    _, hots = head_hots(feats)
    for h in range(EARLY):
        w_ref[h], g_ref[h] = weigh(queries * hots[h], keys, near_count[...], feats // HEADS)


def local_project(x_ref, gain, wq_ref, wk_ref, wv_ref, low_ref):
    xhat, _ = standardize(x_ref[...].astype(F32))
    normed = (xhat * gain).astype(BF16)
    queries = dot(normed, wq_ref[...]).astype(BF16)
    keys = dot(normed, wk_ref[...]).astype(BF16)
    low_ref[0] = queries
    low_ref[1] = keys
    low_ref[2] = dot(normed, wv_ref[...]).astype(BF16)
    low_ref[3] = queries.T
    low_ref[4] = normed.T
    return queries, keys


def local_count(edge_rows, pack_ref, far_count, near_count):
    rows, far = far_count.shape
    edge = 128
    group = 8
    table = pack_ref[4].astype(F32)

    def part(i):
        at = i // 2 * edge_rows
        return table[at : at + edge_rows, i % 2 * edge : (i % 2 + 1) * edge]

    ids = lax.broadcasted_iota(jnp.int32, (rows, edge), 0).astype(F32)

    def hot(values, height, base):
        at = ids[:height]
        return jnp.concatenate(
            [(at == values[j : j + 1]).astype(F32).astype(BF16) for j in range(base, base + group)],
            axis=1,
        )

    row_id = lax.broadcasted_iota(jnp.int32, (rows, rows), 0)
    col_id = lax.broadcasted_iota(jnp.int32, (rows, rows), 1)
    spans = [(b, min(rows, rows + far - b)) for b in range(0, rows + far, rows)]
    totals = [jnp.zeros((rows, height), F32) for _, height in spans]
    totals[0] = (row_id == col_id).astype(F32)
    values = [part(i) for i in range(len(spans) + 1)]
    for base in range(0, edge_rows, group):
        hot_dst = hot(values[0], rows, base)
        for i, (_, height) in enumerate(spans):
            totals[i] = totals[i] + dot_t(hot_dst, hot(values[i + 1], height, base))
    near_count[...] = totals[0]
    for (b, height), total in zip(spans[1:], totals[1:]):
        far_count[:, b - rows : b - rows + height] = total


def attend_kernel(
    edge_rows, far_ref, pack_ref, wo_ref, cot_ref, low_ref, far_count, near_count, near_w, near_g,
    tail_ref, keep_ref, give_ref,
    w_scr, g_scr, far_w, far_g, dkt_scr, dvt_scr,
):
    _, wq_ref, wk_ref, wv_ref = [pack_ref.at[i] for i in range(4)]
    _, rows, feats = low_ref.shape
    queries, keys, values, qt, norm_t = [low_ref[i] for i in range(5)]
    datt = dot_t(cot_ref[...], wo_ref[...]).astype(BF16)
    peers, slots, _ = far_ref.shape
    far = peers * slots
    width = far_count.shape[1]
    head = feats // HEADS
    pairs = HEADS // 2
    chips, block, _ = keep_ref.shape
    pad = width - far
    far_x = jnp.concatenate([far_ref[p].astype(F32) for p in range(peers)], axis=0)
    if pad:
        far_x = jnp.concatenate([far_x, jnp.zeros((pad, feats), F32)], axis=0)
    gain = packed_gain(pack_ref, gain_row(edge_rows, rows, width))
    far_hat, far_rstd = standardize(far_x)
    far_normed = (far_hat * gain).astype(BF16)
    far_keys = dot(far_normed, wk_ref[...]).astype(BF16)
    far_values = dot(far_normed, wv_ref[...]).astype(BF16)
    masks, hots = head_hots(feats)
    lane = lax.broadcasted_iota(jnp.int32, (1, feats), 1)
    even = lax.rem(lane // (2 * head), 2) == 0

    def both(x, j):
        return jnp.concatenate([x * hots[2 * j], x * hots[2 * j + 1]], axis=0)

    def summed(h):
        return hots[h + 2] if h // 2 % 2 == 0 else hots[h - 2]

    count = jnp.concatenate([far_count[...]] * 2, axis=1)
    near = near_count[...]
    seen = [[], []]
    for j in range(pairs):
        w, far_g[j] = weigh(queries, both(far_keys, j), count, head)
        far_w[j] = w
        side = j % 2
        far_ones = jnp.concatenate(
            [jnp.broadcast_to(summed(h), (width, feats)) for h in (2 * j, 2 * j + 1)], axis=0
        )
        seen[side].append((w, both(far_values, j) + far_ones))
        for h in (2 * j, 2 * j + 1):
            if h < EARLY:
                w = near_w[h]
            else:
                w, g_scr[h - EARLY] = weigh(queries * hots[h], keys, near, head)
                w_scr[h - EARLY] = w
            seen[side].append((w, values * hots[h] + summed(h)))
    total = [
        dot(
            jnp.concatenate([w for w, _ in side], axis=1),
            jnp.concatenate([v for _, v in side], axis=0),
        )
        for side in seen
    ]
    num = jnp.where(even, total[0], total[1])
    crossed = jnp.where(even, total[1], total[0])
    den = jnp.concatenate(
        [pltpu.roll(crossed[:, i : i + 4 * head], 2 * head, 1) for i in range(0, feats, 4 * head)],
        axis=1,
    )
    rden = 1.0 / den
    att32 = num * rden
    att = att32.astype(BF16)
    tail_ref[0] = att
    grad_out = dot(att.T, cot_ref[...])
    dnum = (datt.astype(F32) * rden).astype(BF16)
    dnum_t = dnum.T
    prod = dnum.astype(F32) * att32
    dq = jnp.zeros((rows, feats), F32)
    slopes, weights, far_slopes = [], [], []
    for j in range(pairs):
        z = [
            jnp.sum(jnp.where(masks[h], prod, 0.0), axis=1, keepdims=True)
            for h in (2 * j, 2 * j + 1)
        ]
        far_z = jnp.concatenate([jnp.broadcast_to(x, (rows, width)) for x in z], axis=1)
        dw = dot_t(dnum, both(far_values, j)) - far_z
        ds = (far_g[j].astype(F32) * dw).astype(BF16)
        dq = dq + dot(ds, both(far_keys, j))
        far_slopes.append(ds)
        for i, h in enumerate((2 * j, 2 * j + 1)):
            w, g = (near_w[h], near_g[h]) if h < EARLY else (w_scr[h - EARLY], g_scr[h - EARLY])
            dw = dot_t(dnum * hots[h], values) - z[i]
            ds = (g.astype(F32) * dw).astype(BF16)
            dq = dq + dot(ds, keys * hots[h])
            slopes.append(ds)
            weights.append(w)
    for h in range(HEADS):
        at = slice(h * head, (h + 1) * head)
        dkt_scr[at, :rows] = dot(qt[at, :], slopes[h])
        dvt_scr[at, :rows] = dot(dnum_t[at, :], weights[h])
    for j in range(pairs):
        at = slice(2 * j * head, (2 * j + 2) * head)
        dk = dot(qt[at, :], far_slopes[j])
        dv = dot(dnum_t[at, :], far_w[j])
        for i in range(2):
            at = slice((2 * j + i) * head, (2 * j + i + 1) * head)
            part = slice(i * head, (i + 1) * head)
            cols = slice(i * width, (i + 1) * width)
            dkt_scr[at, rows:] = dk[part, cols]
            dvt_scr[at, rows:] = dv[part, cols]
    slope = 1.0 / math.sqrt(head)
    dq = (dq * slope).astype(BF16)
    dkt = (dkt_scr[...] * slope).astype(BF16)
    dvt = dvt_scr[...].astype(BF16)
    tail_ref[1] = dq
    tail_ref[2] = dkt[:, :rows]
    tail_ref[3] = dvt[:, :rows]
    all_t = jnp.concatenate([norm_t, far_normed.T], axis=1)
    grad_query = dot(norm_t, dq)
    grad_key = dot_t(all_t, dkt)
    grad_value = dot_t(all_t, dvt)
    away = (dot(wk_ref[...], dkt[:, rows:]) + dot(wv_ref[...], dvt[:, rows:])).T
    away_dx = pull(away * gain, far_hat, far_rstd)
    share = 2 * feats // chips
    blank = [jnp.zeros((block - share - slots, feats), F32)] * (block > share + slots)
    first = lax.rem(lax.axis_index("nodes"), 2) == 0
    low = jnp.concatenate([grad_query, grad_key], axis=0)
    high = jnp.concatenate([grad_value, grad_out], axis=0)
    keep = jnp.where(first, low, high)
    give = jnp.where(first, high, low)
    for c in range(chips):
        dx = [away_dx[(2 * c + i) * slots : (2 * c + i + 1) * slots] for i in range(2)]
        at = slice(c * share, (c + 1) * share)
        keep_ref[c] = jnp.concatenate(
            [keep[at], jnp.where(first, dx[0], dx[1])] + blank, axis=0
        )
        give_ref[c] = jnp.concatenate(
            [give[at], jnp.where(first, dx[1], dx[0])] + blank, axis=0
        ).astype(BF16)


def pair_kernel(share, slots, keep_ref, got_ref, out_ref):
    chips, block, feats = out_ref.shape
    blank = [jnp.zeros((block - share - 2 * slots, feats), F32)] * (block > share + 2 * slots)
    for c in range(chips):
        keep = keep_ref[c]
        got = got_ref[c].astype(F32)
        end = share + slots
        out_ref[c] = jnp.concatenate(
            [keep[:share] + got[:share], keep[share:end], got[share:end]] + blank, axis=0
        ).astype(BF16)


def reduce_kernel(got_ref, share_ref):
    chips, share, _ = share_ref.shape
    total = jnp.zeros(share_ref.shape[1:], F32)
    for c in range(chips):
        total = total + got_ref[c].astype(F32)[:share]
    share_ref[...] = jnp.broadcast_to(total.astype(BF16)[None], share_ref.shape)


def own_kernel(gain_at, pack_ref, wo_ref, cot_ref, tail_ref, out_ref, feats_ref):
    x_ref, wq_ref, wk_ref, wv_ref = [pack_ref.at[i] for i in range(4)]
    x = x_ref[...].astype(F32)
    out_ref[...] = (x + dot(tail_ref[0], wo_ref[...])).astype(BF16)
    d_normed = (dot(wk_ref[...], tail_ref[2]) + dot(wv_ref[...], tail_ref[3])).T
    d_normed = d_normed + dot_t(tail_ref[1], wq_ref[...])
    gain = packed_gain(pack_ref, gain_at)
    feats_ref[...] = cot_ref[...].astype(F32) + pull(d_normed * gain, *standardize(x))


def finish_kernel(share, send_ref, got_ref, own_ref, feats_ref):
    slots, peers = send_ref.shape
    feats_ref[...] = own_ref[...]
    core = lax.rem(lax.axis_index("nodes"), 2)
    for c in range(peers // 2):
        got = got_ref[c].astype(F32)
        for i in range(2 * slots):
            peer = 2 * c + (core if i < slots else 1 - core)
            at = pl.ds(send_ref[i % slots, peer], 1)
            feats_ref[at, :] += got[share + i : share + i + 1]


def spread_kernel(mine_ref, other_ref, gain_ref, wq_ref, wk_ref, wv_ref, *out_refs):
    rows = wq_ref.shape[0]
    chips, share, feats = mine_ref.shape
    first = lax.rem(lax.axis_index("nodes"), 2) == 0
    mine = mine_ref[...].astype(F32).reshape(chips * share, feats)
    other = other_ref[...].astype(F32).reshape(chips * share, feats)
    low = jnp.where(first, mine, other)
    high = jnp.where(first, other, mine)
    grads = (low[:rows], low[rows:], high[:rows], high[rows:])
    for grad, out_ref in zip(grads, out_refs):
        out_ref[...] = grad
    prod = jnp.zeros((rows, feats), F32)
    for grad, w_ref in zip(grads, (wq_ref, wk_ref, wv_ref)):
        prod = prod + grad * w_ref[...].astype(F32)
    out_refs[4][...] = jnp.sum(prod.T, axis=0, keepdims=True) / gain_ref[...]


def call(kernel, out_shape, in_specs, scratch=(), cost=None, out_specs=None, mib=16):
    return pl.pallas_call(
        kernel,
        out_shape=out_shape,
        in_specs=in_specs,
        out_specs=jax.tree.map(lambda _: VMEM, out_shape) if out_specs is None else out_specs,
        scratch_shapes=list(scratch),
        compiler_params=pltpu.CompilerParams(vmem_limit_bytes=mib * MIB),
        cost_estimate=cost,
    )


def on_device(
    node_feats, norm_gain, w_query, w_key, w_value, w_out, cotangent,
    edge_dst, edge_src, edge_mask, send_rows,
):
    rows, feats = node_feats.shape
    peers, slots = send_rows.shape[1:]
    far = peers * slots
    width = up(far, 128)
    chips = peers // 2
    share = 2 * feats // chips
    block = up(share + slots, 8)
    message = up(share + 2 * slots, 8)
    gain = norm_gain.reshape(1, feats)
    send = send_rows[0].T
    swap = [(i, i ^ 1) for i in range(peers)]
    sides = [list(range(k, peers, 2)) for k in range(2)]

    def like(shape, dtype):
        return jax.ShapeDtypeStruct(shape, dtype)

    def across(x):
        return lax.all_to_all(x, "nodes", 0, 0, axis_index_groups=sides, tiled=True)

    cost = pl.CostEstimate(flops=8_000_000_000, bytes_accessed=2_000_000, transcendentals=0)
    square = like((rows, feats), BF16)
    wide = like((rows, feats), F32)
    edges = edge_dst.shape
    picked, pack = call(
        pick_kernel,
        (like((peers, slots, feats), BF16), like((5, rows, feats), BF16)),
        [SMEM] + [VMEM] * 8,
        (pltpu.VMEM((rows, feats), F32),),
        mib=FULL,
    )(send, node_feats, w_query, w_key, w_value, edge_dst, edge_src, edge_mask, gain)
    arrived = lax.all_to_all(picked, "nodes", split_axis=0, concat_axis=0, tiled=True)
    heads = like((EARLY, rows, rows), BF16)
    low, far_count, near_count, w, g = call(
        functools.partial(local_kernel, edges[0]),
        (like((5, rows, feats), BF16), like((rows, width), F32), like((rows, rows), F32),
         heads, heads),
        [VMEM],
        cost=cost,
    )(pack)
    late = pltpu.VMEM((max(HEADS - EARLY, 1), rows, rows), BF16)
    far_heads = pltpu.VMEM((HEADS // 2, rows, 2 * width), BF16)
    turned = pltpu.VMEM((feats, rows + width), F32)
    tail, keep, give = call(
        functools.partial(attend_kernel, edges[0]),
        (like((4, rows, feats), BF16), like((chips, block, feats), F32),
         like((chips, block, feats), BF16)),
        [VMEM] * 9,
        [late, late, far_heads, far_heads, turned, turned],
    )(arrived, pack, w_out, cotangent, low, far_count, near_count, w, g)
    given = lax.ppermute(give, "nodes", swap)
    output, own = call(
        functools.partial(own_kernel, gain_row(edges[0], rows, width)),
        (square, wide),
        [VMEM] * 4,
        cost=cost,
    )(pack, w_out, cotangent, tail)
    given, own = lax.optimization_barrier((given, own))
    paired = call(
        functools.partial(pair_kernel, share, slots),
        like((chips, message, feats), BF16),
        [VMEM] * 2,
    )(keep, given)
    got = across(paired)
    shares = call(reduce_kernel, like((chips, share, feats), BF16), [VMEM])(got)
    mine = across(shares)
    other = lax.ppermute(mine, "nodes", swap)
    grad_feats = call(
        functools.partial(finish_kernel, share), wide, [SMEM] + [VMEM] * 2, cost=cost
    )(send, got, own)
    *grads, grad_gain = call(
        spread_kernel, (like((feats, feats), F32),) * 4 + (like((1, feats), F32),), [VMEM] * 6
    )(mine, other, gain, w_query, w_key, w_value)
    return (output, grad_feats, grad_gain.reshape(feats), *grads)


def solution(mesh):
    nodes = P(("groups", "nodes"), None)
    in_specs = (
        nodes, P(), P(), P(), P(), P(), nodes, nodes, nodes, nodes,
        P(("groups", "nodes"), None, None),
    )
    out_specs = (nodes, nodes, P("groups")) + (P("groups", None),) * 4
    return jax.shard_map(
        on_device, mesh=mesh, in_specs=in_specs, out_specs=out_specs, check_vma=False
    )
```
